512 devices in a mesh: dp: 64 (over z_hi, y, x), tensor: 8 (over z_lo, core).
Axes of the slice: x: 4, y: 8, z: 8 (z_hi: 2, z_lo: 4; z = z_hi * 4 + z_lo), core: 2. Of those that a mesh axis runs over, the one named last changes fastest.
Arguments:
- frames: bfloat16 [16384, 1536], P('dp', 'tensor'), may hold values from -6 to 6
- norm_gain: float32 [1536], replicated, may hold values from 0.5 to 2
- norm_bias: float32 [1536], replicated, may hold values from -3 to 3
- input_weight: bfloat16 [2, 1536, 1536], P(None, 'tensor'), may hold values from -0.15625 to 0.15625
- depth_weight: float32 [32, 1536], P(None, 'tensor'), may hold values from -1.5 to 1.5
- batch_scale: float32 [1536], P('tensor'), may hold values from 0.5 to 2
- batch_shift: float32 [1536], P('tensor'), may hold values from -3 to 3
- output_weight: bfloat16 [1536, 1536], P('tensor'), may hold values from -0.15625 to 0.15625
- upstream: bfloat16 [32768, 1536], P(('dp', 'tensor')), may hold values from -6 to 6
- replica_blocks: int32 [64], replicated, may hold values from 0 to 64, as said below
- segment: int32 [32768], P('dp'), may hold values from 0 to 32, as said below
Outputs:
- block_output: bfloat16 [32768, 1536], P(('dp', 'tensor'))
- frame_gradient: bfloat16 [16384, 1536], P('dp', 'tensor')
- input_weight_gradient: bfloat16 [2, 1536, 1536], P(None, 'tensor')
- output_weight_gradient: bfloat16 [1536, 1536], P('tensor')
- depth_weight_gradient: float32 [32, 1536], P(None, 'tensor')
- gain_gradient: float32 [1536], P('tensor')
- bias_gradient: float32 [1536], P('tensor')
The draws below stay inside these ranges and needn't reach their ends.
Inputs may be any that keep to these rules, and one draw needn't show every extreme that they name: `replica_blocks`: the counts sum to 2048. `segment`: within a replica's 512 slots the number starts at 0 and never falls.
All inputs are finite; a program needn't handle non-finite values.
Results may differ from the reference program's by a relative error of at most 0.017.
Values may be sent and summed in bfloat16 or wider, within the bound.
No kernel may reach another device: no remote copies, remote signals or barrier semaphores. Data moves between devices by JAX's collectives and lax.ppermute only.
A program may use at most 64 MiB of HBM per device.

```python
import math
import jax
import jax.numpy as jnp
from jax import lax

D = 1536
KERNEL = 32
BLK = 8
LOAD_DEV = 256
FR_DEV = 512
LOADED = 16384
TOKENS = 32768
N_DP = 64
N_TENSOR = 8


def draw_replica_blocks(key, part):
    key = jax.random.fold_in(key, 11)
    perm_key, move_key = jax.random.split(key)
    load_blocks = LOAD_DEV // BLK
    order = jax.random.permutation(perm_key, N_DP).astype(jnp.int32)
    moved = jax.random.randint(move_key, (N_DP // 2,), 0, load_blocks + 1).astype(jnp.int32)
    moved = moved.at[0].set(load_blocks)
    counts = jnp.zeros((N_DP,), jnp.int32)
    counts = counts.at[order[0::2]].set(load_blocks + moved)
    counts = counts.at[order[1::2]].set(load_blocks - moved)
    return counts


def draw_segment(key, part):
    key = jax.random.fold_in(key, 23)
    marks = (jax.random.randint(key, (N_DP, FR_DEV), 0, 64) == 0).astype(jnp.int32)
    every_eighth = (jnp.arange(FR_DEV, dtype=jnp.int32) % 8 == 0).astype(jnp.int32)
    marks = marks.at[0].set(jnp.maximum(marks[0], every_eighth))
    marks = marks.at[:, 0].set(0)
    counted = jnp.cumsum(marks, axis=1).astype(jnp.int32)
    return jnp.minimum(counted, FR_DEV // 16).astype(jnp.int32).reshape(-1)


def levels(own_key, extent, cuts, smallest, top_value):
    def one(axis_at, blocks):
        heights = jax.random.uniform(jax.random.fold_in(jax.random.fold_in(own_key, 6), axis_at), (blocks,), jnp.float32, smallest / len(cuts), top_value / len(cuts))
        return jnp.repeat(jnp.exp(heights), extent[axis_at] // blocks).reshape((-1,) + (1,) * (len(extent) - axis_at - 1))

    factor_of = one(*cuts[0])
    for cut in cuts[1:]:
        factor_of = factor_of * one(*cut)
    return factor_of


def noise(stream_key, shape, scale, limit, shards=(), kind=jnp.bfloat16):
    loudness = levels(stream_key, shape, shards, -0.22, 0.18) if shards else 1.0
    drawn = jax.random.normal(stream_key, shape, jnp.float32) * scale * loudness
    return jnp.minimum(jnp.maximum(drawn, -limit), limit).astype(kind)


def setup_inputs(seed: int = 0) -> dict:
    key_of = jax.random.split(jax.random.key(seed), 12)
    return {
        "frames": noise(key_of[0], (LOADED, D), 1.0, 6.0, ((0, 64), (1, 8))),
        "norm_gain": jnp.clip(jnp.exp(jax.random.uniform(key_of[1], (D,), jnp.float32, math.log(0.5), math.log(2.0))), 0.5, 2.0),
        "norm_bias": noise(key_of[2], (D,), 0.5, 3.0, (), jnp.float32),
        "input_weight": noise(key_of[3], (2, D, D), D ** -0.5, 0.15625, ((1, 8),)),
        "depth_weight": noise(key_of[4], (KERNEL, D), (KERNEL // 2) ** -0.5, 1.5, ((1, 8),), jnp.float32),
        "batch_scale": jnp.clip(jnp.exp(math.log(2.0) - 1.3862944 * jax.random.uniform(key_of[5], (D,), jnp.float32) ** levels(key_of[5], (D,), ((0, 8),), -0.2, 0.2)), 0.5, 2.0),
        "batch_shift": noise(key_of[6], (D,), 0.5, 3.0, ((0, 8),), jnp.float32),
        "output_weight": noise(key_of[7], (D, D), D ** -0.5, 0.15625, ((0, 8),)),
        "upstream": noise(key_of[8], (TOKENS, D), 1.0, 6.0, ((0, 512),)),
        "replica_blocks": draw_replica_blocks(jax.random.fold_in(key_of[11], 71), 0),
        "segment": draw_segment(jax.random.fold_in(key_of[11], 71), 0),
    }


epsilon = 1e-05

def rounded(value):
    return lax.optimization_barrier(value.astype(jnp.bfloat16)).astype(jnp.float32)

def reference(frames, norm_gain, norm_bias, input_weight, depth_weight, batch_scale, batch_shift, output_weight, upstream, replica_blocks, segment):
    load_blocks = LOAD_DEV // BLK
    cap_blocks = 2 * load_blocks
    row_count = FR_DEV
    group = D // N_TENSOR
    run_ends = jnp.cumsum(replica_blocks).astype(jnp.int32)
    starts = (run_ends - replica_blocks).astype(jnp.int32)
    numbers = jnp.arange(N_DP * load_blocks, dtype=jnp.int32)
    loader = numbers % N_DP
    turn = numbers // N_DP
    target = lax.optimization_barrier(jnp.sum((run_ends[None, :] <= numbers[:, None]).astype(jnp.int32), axis=1)).astype(jnp.int32)
    position = numbers - starts[target]
    source_block = (loader * load_blocks + turn).astype(jnp.int32)
    slot_block = (target * cap_blocks + position).astype(jnp.int32)
    block_view = frames.reshape(N_DP * load_blocks, BLK, D)
    packed = jnp.zeros((N_DP * cap_blocks, BLK, D), jnp.bfloat16).at[slot_block].set(block_view[source_block])
    x_rows = packed.reshape(N_DP, row_count, D)
    active = (jnp.arange(row_count, dtype=jnp.int32) // BLK)[None, :] < replica_blocks[:, None]
    seg_rows = segment.reshape(N_DP, row_count)
    x_float = x_rows.astype(jnp.float32)
    center = lax.optimization_barrier(jnp.mean(x_float, axis=-1, keepdims=True))
    spread = lax.optimization_barrier(jnp.mean(jnp.square(x_float - center), axis=-1, keepdims=True))
    scale_row = lax.rsqrt(spread + epsilon)
    standard = (x_float - center) * scale_row
    normed = (standard * norm_gain + norm_bias).astype(jnp.bfloat16)
    flat_normed = normed.reshape(-1, D)
    linear = jnp.dot(flat_normed, input_weight[0].T, preferred_element_type=jnp.float32).reshape(N_DP, row_count, D)
    gate = jnp.dot(flat_normed, input_weight[1].T, preferred_element_type=jnp.float32).reshape(N_DP, row_count, D)
    gate_sigmoid = jax.nn.sigmoid(gate)
    glu = (linear * gate_sigmoid).astype(jnp.bfloat16)
    front = KERNEL // 2
    back = KERNEL - 1 - front
    seg_pad = jnp.pad(seg_rows, ((0, 0), (front, back)), constant_values=-1)
    active_pad = jnp.pad(active, ((0, 0), (front, back)))
    glu_pad = jnp.pad(glu, ((0, 0), (front, back), (0, 0)))
    tap_masks = []
    for offset in range(KERNEL):
        same = (seg_pad[:, offset:offset + row_count] == seg_rows) & active_pad[:, offset:offset + row_count]
        tap_masks.append(same.astype(jnp.float32)[:, :, None])
    conv_sum = jnp.zeros((N_DP, row_count, D), jnp.float32)
    for offset in range(KERNEL):
        conv_sum = conv_sum + depth_weight[offset] * glu_pad[:, offset:offset + row_count].astype(jnp.float32) * tap_masks[offset]
    preswish = conv_sum * batch_scale + batch_shift
    pre_sigmoid = jax.nn.sigmoid(preswish)
    swish = (preswish * pre_sigmoid).astype(jnp.bfloat16)
    flat_swish = swish.reshape(-1, D)
    mixed_sum = jnp.zeros((N_DP * row_count, D), jnp.float32)
    for index in range(N_TENSOR):
        lower = index * group
        term = jnp.dot(flat_swish[:, lower:lower + group], output_weight[lower:lower + group], preferred_element_type=jnp.float32)
        mixed_sum = mixed_sum + rounded(term)
    mixed_sum = mixed_sum.reshape(N_DP, row_count, D)
    active_col = active[:, :, None]
    block_output = jnp.where(active_col, x_float + mixed_sum, 0.0).astype(jnp.bfloat16)
    cotangent = upstream.reshape(N_DP, row_count, D)
    delta_out = jnp.where(active_col, cotangent, jnp.zeros_like(cotangent))
    flat_delta = delta_out.reshape(-1, D)
    delta_swish = jnp.dot(flat_delta, output_weight.T, preferred_element_type=jnp.float32).reshape(N_DP, row_count, D)
    output_weight_gradient = jnp.dot(flat_swish.T, flat_delta, preferred_element_type=jnp.float32).astype(jnp.bfloat16)
    delta_conv = delta_swish * pre_sigmoid * (1.0 + preswish * (1.0 - pre_sigmoid)) * batch_scale
    delta_pad = jnp.zeros((N_DP, row_count + KERNEL - 1, D), jnp.float32)
    tap_rows = []
    for offset in range(KERNEL):
        contrib = delta_conv * tap_masks[offset]
        delta_pad = delta_pad.at[:, offset:offset + row_count].add(depth_weight[offset] * contrib)
        tap_rows.append(lax.optimization_barrier(jnp.sum(contrib * glu_pad[:, offset:offset + row_count].astype(jnp.float32), axis=(0, 1))))
    delta_glu = delta_pad[:, front:front + row_count]
    depth_weight_gradient = jnp.stack(tap_rows)
    delta_linear = (delta_glu * gate_sigmoid).astype(jnp.bfloat16).reshape(-1, D)
    delta_gate = (delta_glu * linear * gate_sigmoid * (1.0 - gate_sigmoid)).astype(jnp.bfloat16).reshape(-1, D)
    input_weight_gradient = jnp.stack([jnp.dot(delta_linear.T, flat_normed, preferred_element_type=jnp.float32), jnp.dot(delta_gate.T, flat_normed, preferred_element_type=jnp.float32)]).astype(jnp.bfloat16)
    delta_normed = jnp.zeros((N_DP * row_count, D), jnp.float32)
    for index in range(N_TENSOR):
        lower = index * group
        term = jnp.dot(delta_linear[:, lower:lower + group], input_weight[0][lower:lower + group], preferred_element_type=jnp.float32)
        term = term + jnp.dot(delta_gate[:, lower:lower + group], input_weight[1][lower:lower + group], preferred_element_type=jnp.float32)
        delta_normed = delta_normed + rounded(term)
    delta_normed = delta_normed.reshape(N_DP, row_count, D)
    gain_gradient = lax.optimization_barrier(jnp.sum(delta_normed * standard, axis=(0, 1)))
    bias_gradient = lax.optimization_barrier(jnp.sum(delta_normed, axis=(0, 1)))
    delta_standard = delta_normed * norm_gain
    delta_x = delta_out.astype(jnp.float32) + scale_row * (delta_standard - lax.optimization_barrier(jnp.mean(delta_standard, axis=-1, keepdims=True)) - standard * lax.optimization_barrier(jnp.mean(delta_standard * standard, axis=-1, keepdims=True)))
    delta_blocks = delta_x.astype(jnp.bfloat16).reshape(N_DP * cap_blocks, BLK, D)
    frame_gradient = jnp.zeros((N_DP * load_blocks, BLK, D), jnp.bfloat16).at[source_block].set(delta_blocks[slot_block]).reshape(N_DP * LOAD_DEV, D)
    return (block_output.reshape(N_DP * row_count, D), frame_gradient, input_weight_gradient, output_weight_gradient, depth_weight_gradient, gain_gradient, bias_gradient)
```

```python
import functools

import jax
import jax.numpy as jnp
from jax import lax
from jax.experimental import pallas as pl
from jax.experimental.pallas import tpu as pltpu
from jax.sharding import Mesh
from jax.sharding import PartitionSpec as P

BLK = 8
LANES = 128
EDGE = 16
epsilon = 1e-05
VMEM_LIMIT = 40 * 1024 * 1024

f32 = jnp.float32
bf16 = jnp.bfloat16
DP = ("zh", "y", "x")
TENSOR = ("zl", "core")


def dot_general(a, b, ca, cb):
    return lax.dot_general(a, b, (((ca,), (cb,)), ((), ())), preferred_element_type=f32)


def full_call(kernel, out_shape, scratch, smem, flops, nbytes):
    def call(*args):
        specs = [pl.BlockSpec(memory_space=pltpu.SMEM)] * smem
        specs += [pl.BlockSpec(memory_space=pltpu.VMEM)] * (len(args) - smem)
        outs = jax.tree.map(lambda _: pl.BlockSpec(memory_space=pltpu.VMEM), out_shape)
        return pl.pallas_call(
            kernel,
            out_shape=out_shape,
            in_specs=specs,
            out_specs=outs,
            scratch_shapes=scratch,
            compiler_params=pltpu.CompilerParams(vmem_limit_bytes=VMEM_LIMIT),
            cost_estimate=pl.CostEstimate(flops=flops, bytes_accessed=nbytes, transcendentals=0),
        )(*args)

    return call


def pack_kernel(scalars, arrived, rows_out, cols_out, held):
    start, blocks = scalars[0], scalars[1]
    count, _, width = arrived.shape
    for p in range(count):
        block = arrived[lax.rem(start + p, count)].astype(f32)
        held[p * BLK : (p + 1) * BLK, :] = jnp.where(p < blocks, block, 0.0)
    rows = held[...]
    rows_out[...] = rows.astype(bf16)
    for c in range(0, width, LANES):
        e = min(width, c + LANES)
        cols_out[c:e, :] = jnp.transpose(held[:, c:e]).astype(bf16)


def shift_masks(seg_s, base, offset, step, rows):
    return seg_s[pl.ds(base + offset, rows), :] == seg_s[pl.ds(base + EDGE, rows), :]


def main_kernel(
    scalars,
    x_ref,
    gb_ref,
    win_ref,
    taps_ref,
    scale_ref,
    shift_ref,
    seg_ref,
    delta_ref,
    wout_ref,
    normed_ref,
    swish_ref,
    dlt_ref,
    back_ref,
    tap_ref,
    stats_ref,
    totals_ref,
    glu_s,
    dc_s,
    seg_s,
    w_s,
    bn_s,
    pre_s,
    dglu_s,
    lin_s,
    sig_s,
    tap_s,
):
    width, slots = x_ref.shape
    part = win_ref.shape[1]
    taps = taps_ref.shape[0]
    rest = part - LANES
    live = scalars[1] * BLK
    chunk = 64
    steps = width // chunk

    def fold(v):
        return jnp.sum(v.reshape(chunk // BLK, BLK, slots), axis=0)

    def sum_body(i, acc):
        return acc + fold(x_ref[pl.ds(i * chunk, chunk), :].astype(f32))

    zero = jnp.zeros((BLK, slots), f32)
    center = jnp.sum(lax.fori_loop(0, steps, sum_body, zero, unroll=2), axis=0, keepdims=True) / width

    def square_body(i, acc):
        return acc + fold(jnp.square(x_ref[pl.ds(i * chunk, chunk), :].astype(f32) - center))

    spread = jnp.sum(lax.fori_loop(0, steps, square_body, zero, unroll=2), axis=0, keepdims=True) / width
    row_scale = lax.rsqrt(spread + epsilon)
    stats_ref[...] = jnp.zeros_like(stats_ref)
    stats_ref[0:1, :] = center
    stats_ref[1:2, :] = row_scale

    def norm_body(i, carry):
        at = pl.ds(i * chunk, chunk)
        standard = (x_ref[at, :].astype(f32) - center) * row_scale
        normed_ref[at, :] = (standard * gb_ref[at, 0:1] + gb_ref[at, 1:2]).astype(bf16)
        return carry

    lax.fori_loop(0, steps, norm_body, 0, unroll=2)

    glu_s[...] = jnp.zeros_like(glu_s)
    dc_s[...] = jnp.zeros_like(dc_s)
    normed = normed_ref[...]
    linear = dot_general(win_ref[0], normed, 1, 0)
    gate_sigmoid = jax.nn.sigmoid(dot_general(win_ref[1], normed, 1, 0))
    lin_s[...] = linear
    sig_s[...] = gate_sigmoid
    is_live = lax.broadcasted_iota(jnp.int32, (part, slots), 1) < live
    glu = jnp.where(is_live, (linear * gate_sigmoid).astype(bf16).astype(f32), 0.0)
    glu_s[0, EDGE : EDGE + slots, :] = jnp.transpose(glu[0:LANES])
    glu_s[1, EDGE : EDGE + slots, 0:rest] = jnp.transpose(glu[LANES:part])

    w_s[...] = jnp.zeros_like(w_s)
    w_s[0] = taps_ref[:, 0:LANES]
    w_s[1, :, 0:rest] = taps_ref[:, LANES:part]
    bn_s[...] = jnp.zeros_like(bn_s)
    bn_s[0, 0:1, :] = scale_ref[:, 0:LANES]
    bn_s[1, 0:1, 0:rest] = scale_ref[:, LANES:part]
    bn_s[0, 1:2, :] = shift_ref[:, 0:LANES]
    bn_s[1, 1:2, 0:rest] = shift_ref[:, LANES:part]
    seg_s[...] = jnp.full(seg_s.shape, -1, jnp.int32)
    seg_s[EDGE : EDGE + slots, :] = jnp.broadcast_to(seg_ref[...], (slots, LANES))

    rows = 64
    blocks = slots // rows

    def conv_body(i, carry):
        base = pl.multiple_of(i * rows, rows)
        here = seg_s[pl.ds(base + EDGE, rows), :]
        acc = [jnp.zeros((rows, LANES), f32) for _ in range(2)]
        for j in range(taps):
            same = seg_s[pl.ds(base + j, rows), :] == here
            for h in range(2):
                value = jnp.where(same, glu_s[h, pl.ds(base + j, rows), :], 0.0)
                acc[h] = acc[h] + value * w_s[h, j : j + 1, :]
        for h in range(2):
            pre_s[h, pl.ds(base, rows), :] = acc[h] * bn_s[h, 0:1, :] + bn_s[h, 1:2, :]
        return carry

    lax.fori_loop(0, blocks, conv_body, 0)

    delta_swish = dot_general(delta_ref[...], wout_ref[...], 1, 1)
    row_live = lax.broadcasted_iota(jnp.int32, (slots, LANES), 0) < live
    for h in range(2):
        pre = pre_s[h]
        s = jax.nn.sigmoid(pre)
        swish = jnp.where(row_live, pre * s, 0.0).astype(bf16)
        slope = jnp.where(row_live, s * (1.0 + pre * (1.0 - s)) * bn_s[h, 0:1, :], 0.0)
        if h == 0:
            swish_ref[:, 0:LANES] = swish
            dc_s[h, EDGE : EDGE + slots, :] = delta_swish[:, 0:LANES] * slope
        else:
            swish_ref[:, LANES:part] = swish[:, 0:rest]
            dc_s[h, EDGE : EDGE + slots, 0:rest] = delta_swish[:, LANES:part] * slope[:, 0:rest]

    tap_s[...] = jnp.zeros_like(tap_s)

    def back_body(i, carry):
        base = pl.multiple_of(i * rows, rows)
        here = seg_s[pl.ds(base + EDGE, rows), :]
        alive = (base + lax.broadcasted_iota(jnp.int32, (rows, LANES), 0)) < live
        glu_here = [glu_s[h, pl.ds(base + EDGE, rows), :] for h in range(2)]
        acc = [jnp.zeros((rows, LANES), f32) for _ in range(2)]
        for j in range(taps):
            at = pl.ds(base + (2 * EDGE - j), rows)
            same = seg_s[at, :] == here
            for h in range(2):
                value = jnp.where(same, dc_s[h, at, :], 0.0)
                acc[h] = acc[h] + value * w_s[h, j : j + 1, :]
                tap_s[h, j] += jnp.sum((value * glu_here[h]).reshape(rows // BLK, BLK, LANES), axis=0)
        for h in range(2):
            dglu_s[h, pl.ds(base, rows), :] = jnp.where(alive, acc[h], 0.0)
        return carry

    lax.fori_loop(0, blocks, back_body, 0)
    for h in range(2):
        tap_ref[h] = jnp.sum(tap_s[h], axis=1)

    for h, (c, e) in enumerate(((0, LANES), (LANES, part))):
        dglu = jnp.transpose(dglu_s[h])[0 : e - c]
        s = sig_s[c:e, :]
        dlt_ref[0, c:e, :] = (dglu * s).astype(bf16)
        dlt_ref[1, c:e, :] = (dglu * lin_s[c:e, :] * s * (1.0 - s)).astype(bf16)

    unit = jnp.zeros((BLK, slots), f32)
    cross = jnp.zeros((BLK, slots), f32)
    wide = 256
    for d in range(0, width, wide):
        term = dot_general(win_ref[0, :, d : d + wide], dlt_ref[0], 0, 0)
        term = term + dot_general(win_ref[1, :, d : d + wide], dlt_ref[1], 0, 0)
        term = term.astype(bf16)
        back_ref[d : d + wide, :] = term
        weighted = term.astype(f32) * gb_ref[d : d + wide, 0:1]
        standard = (x_ref[d : d + wide, :].astype(f32) - center) * row_scale
        unit = unit + jnp.sum(weighted.reshape(wide // BLK, BLK, slots), axis=0)
        cross = cross + jnp.sum((weighted * standard).reshape(wide // BLK, BLK, slots), axis=0)
    totals_ref[0:1, :] = jnp.sum(unit, axis=0, keepdims=True)
    totals_ref[1:2, :] = jnp.sum(cross, axis=0, keepdims=True)


def weight_kernel(normed_ref, swish_ref, dlt_ref, delta_ref, wout_ref, tap_ref, mixed_ref, grad_ref):
    width = normed_ref.shape[0]
    part = swish_ref.shape[1]
    taps = tap_ref.shape[1]
    rest = part - LANES
    pieces = grad_ref.shape[0]
    per = part // BLK
    extra = grad_ref.shape[2] - width
    cols = 512
    mixed_ref[...] = dot_general(swish_ref[...], wout_ref[...], 1, 0).astype(bf16)
    swish_t = jnp.transpose(swish_ref[...].astype(f32)).astype(bf16)
    for d in range(0, width, cols):
        for k in range(2):
            block = dot_general(dlt_ref[k], normed_ref[d : d + cols, :], 1, 1).astype(bf16)
            grad_ref[k * per : (k + 1) * per, :, d : d + cols] = block.reshape(per, BLK, cols)
        block = dot_general(swish_t, delta_ref[:, d : d + cols], 1, 0).astype(bf16)
        left = pieces - 2 * per
        grad_ref[2 * per : pieces, :, d : d + cols] = block[0 : left * BLK].reshape(left, BLK, cols)
        over = block[left * BLK :].reshape(per - left, BLK, cols)
        for r in range(per - left):
            for c in range(0, cols, extra):
                at = r * (width // extra) + (d + c) // extra
                grad_ref[at, :, width : width + extra] = over[r, :, c : c + extra]
    first = (per - left) * (width // extra)
    grad_ref[first:pieces, :, width : width + extra] = jnp.zeros((pieces - first, BLK, extra), bf16)
    for r in range(taps // BLK):
        at = slice(r * BLK, (r + 1) * BLK)
        grad_ref[first + r, :, width : width + LANES] = tap_ref[0, at, :].astype(bf16)
        grad_ref[first + r, :, width + LANES : width + part] = tap_ref[1, at, 0:rest].astype(bf16)


def row_kernel(scalars, dn_ref, x_ref, stats_ref, totals_ref, gain_ref, delta_ref, out_ref, held):
    start, blocks = scalars[0], scalars[1]
    part, slots = dn_ref.shape
    width = scalars[2].astype(f32)
    rest = part - LANES
    count = slots // BLK
    live = blocks * BLK
    side = jnp.concatenate([stats_ref[0:2, :], totals_ref[...], jnp.zeros((4, slots), f32)], axis=0)
    side = jnp.transpose(side)
    center, row_scale = side[:, 0:1], side[:, 1:2]
    unit, cross = side[:, 2:3] / width, side[:, 3:4] / width
    sums = []
    for h, (c, e) in enumerate(((0, LANES), (LANES, part))):
        dn = jnp.transpose(dn_ref[c:e, :].astype(f32))
        standard = (x_ref[:, c:e].astype(f32) - center) * row_scale
        sums.append((jnp.sum(dn * standard, axis=0, keepdims=True), jnp.sum(dn, axis=0, keepdims=True)))
        on = lax.broadcasted_iota(jnp.int32, (slots, e - c), 0) < live
        own = jnp.where(on, delta_ref[:, c:e].astype(f32), 0.0)
        held[h, :, 0 : e - c] = own + row_scale * (dn * gain_ref[:, c:e] - unit - standard * cross)
    held[1, :, rest:LANES] = jnp.zeros((slots, LANES - rest), f32)
    row = lax.broadcasted_iota(jnp.int32, (BLK, LANES), 0)
    lane = lax.broadcasted_iota(jnp.int32, (BLK, LANES), 1)
    beside = jnp.zeros((BLK, LANES), f32)
    for k in range(2):
        low = jnp.broadcast_to(sums[0][k], (BLK, LANES))
        high = jnp.broadcast_to(jnp.concatenate([sums[1][k], sums[1][k]], axis=1), (BLK, LANES))
        beside = jnp.where(row == 3 * k, pltpu.roll(low, 64, 1), beside)
        beside = jnp.where(row == 3 * k + 1, low, beside)
        beside = jnp.where(row == 3 * k + 2, high, beside)
    for s in range(count):
        at = pl.ds(pl.multiple_of(lax.rem(s - start + 16 * count, count) * BLK, BLK), BLK)
        out_ref[s, :, 0:LANES] = held[0, at, :].astype(bf16)
        out_ref[s, :, LANES : 2 * LANES] = jnp.where(lane < rest, held[1, at, :], beside).astype(bf16)


def on_device(
    frames,
    norm_gain,
    norm_bias,
    input_weight,
    depth_weight,
    batch_scale,
    batch_shift,
    output_weight,
    upstream,
    replica_blocks,
    segment,
):
    replicas = lax.axis_size(DP)
    my_index = lax.axis_index(DP)
    tensor_index = lax.axis_index(TENSOR)
    width = norm_gain.shape[0]
    load_rows, part = frames.shape
    slots = segment.shape[0]
    rows_part = upstream.shape[0]
    taps = depth_weight.shape[0]
    load_blocks = load_rows // BLK
    count = slots // BLK

    delta = lax.all_gather(upstream, TENSOR, axis=0, tiled=True)

    ends = jnp.cumsum(replica_blocks)
    starts = ends - replica_blocks
    send = jnp.clip((starts - my_index + replicas - 1) // replicas, 0, load_blocks - 1)
    numbers = my_index + replicas * jnp.arange(load_blocks, dtype=jnp.int32)
    target = jnp.sum((ends[None, :] <= numbers[:, None]).astype(jnp.int32), axis=1)
    is_mine = jnp.arange(replicas, dtype=jnp.int32) == my_index
    my_start = jnp.sum(jnp.where(is_mine, starts, 0))
    my_blocks = jnp.sum(jnp.where(is_mine, replica_blocks, 0))
    scalars = jnp.stack([lax.rem(my_start, replicas), my_blocks, jnp.int32(width)])

    outbox = frames.reshape(load_blocks, BLK, part)[send]
    arrived = lax.all_to_all(outbox, DP, split_axis=0, concat_axis=0, tiled=True)

    sds = jax.ShapeDtypeStruct
    packed, packed_t = full_call(
        pack_kernel,
        (sds((slots, part), bf16), sds((part, slots), bf16)),
        [pltpu.VMEM((slots, part), f32)],
        1,
        1000,
        1000000,
    )(scalars, arrived)
    gathered = lax.all_gather(packed_t, TENSOR, axis=0, tiled=True)

    both = jnp.stack([norm_gain, norm_bias], axis=1)
    normed, swish, dlt, back, tap, stats, totals = full_call(
        main_kernel,
        (
            sds((width, slots), bf16),
            sds((slots, part), bf16),
            sds((2, part, slots), bf16),
            sds((width, slots), bf16),
            sds((2, taps, LANES), f32),
            sds((BLK, slots), f32),
            sds((2, slots), f32),
        ),
        [
            pltpu.VMEM((2, slots + 2 * EDGE, LANES), f32),
            pltpu.VMEM((2, slots + 2 * EDGE, LANES), f32),
            pltpu.VMEM((slots + 2 * EDGE, LANES), jnp.int32),
            pltpu.VMEM((2, taps, LANES), f32),
            pltpu.VMEM((2, BLK, LANES), f32),
            pltpu.VMEM((2, slots, LANES), f32),
            pltpu.VMEM((2, slots, LANES), f32),
            pltpu.VMEM((part, slots), f32),
            pltpu.VMEM((part, slots), f32),
            pltpu.VMEM((2, taps, BLK, LANES), f32),
        ],
        1,
        2000000000,
        10000000,
    )(
        scalars,
        gathered,
        both,
        input_weight,
        depth_weight,
        batch_scale[None],
        batch_shift[None],
        segment[:, None],
        delta,
        output_weight,
    )
    delta_normed = lax.psum_scatter(back, TENSOR, scatter_dimension=0, tiled=True)
    totals = lax.psum(totals, TENSOR)

    pieces = replicas
    mixed, grads = full_call(
        weight_kernel,
        (sds((slots, width), bf16), sds((pieces, BLK, width + 2 * LANES), bf16)),
        [],
        0,
        1500000000,
        8000000,
    )(normed, swish, dlt, delta, output_weight, tap)
    mixed_sum = lax.psum_scatter(mixed, TENSOR, scatter_dimension=0, tiled=True)

    grads = lax.all_to_all(grads, DP, split_axis=0, concat_axis=0, tiled=True)
    mine = jnp.sum(grads.astype(f32), axis=0).astype(bf16)
    spread = jnp.broadcast_to(mine[None], (pieces,) + mine.shape)

    column_start = tensor_index * part
    gain_part = lax.dynamic_slice_in_dim(norm_gain, column_start, part)[None]
    delta_part = lax.dynamic_slice_in_dim(delta, column_start, part, 1)
    homebound = full_call(
        row_kernel,
        sds((count, BLK, 2 * LANES), bf16),
        [pltpu.VMEM((2, slots, LANES), f32)],
        1,
        1000000,
        1000000,
    )(scalars, delta_normed, packed, stats, totals, gain_part, delta_part)
    returned = lax.all_to_all(homebound, DP, split_axis=0, concat_axis=0, tiled=True)
    frame_gradient = returned[target][:, :, :part].reshape(load_rows, part)
    side = jnp.sum(returned[:, 0:6, part:].astype(f32), axis=0).reshape(2, part)

    whole = lax.all_to_all(spread, DP, split_axis=0, concat_axis=0, tiled=True)
    per = part // BLK
    weight_grad = whole[: 2 * per, :, :width].reshape(2, part, width)
    over = whole[: 2 * per, :, width:].reshape(BLK, 6, BLK, 2 * LANES)
    over = over.transpose(0, 2, 1, 3).reshape(BLK * BLK, width)
    out_grad = jnp.concatenate([whole[2 * per :, :, :width].reshape(-1, width), over], axis=0)
    tap_grad = whole[2 * per : 2 * per + taps // BLK, :, width : width + part]
    tap_grad = tap_grad.reshape(taps, part).astype(f32)

    row_start = tensor_index * rows_part
    live_mine = (row_start + jnp.arange(rows_part, dtype=jnp.int32) < my_blocks * BLK)[:, None]
    residual = lax.dynamic_slice_in_dim(gathered, row_start, rows_part, 1).T
    block_output = jnp.where(
        live_mine, residual.astype(f32) + mixed_sum.astype(f32), 0.0
    ).astype(bf16)
    return (block_output, frame_gradient, weight_grad, out_grad, tap_grad, side[0], side[1])


def solution(mesh):
    fine = Mesh(mesh.devices.reshape(2, 8, 4, 4, 2), DP + TENSOR)
    in_specs = (
        P(DP, TENSOR),
        P(),
        P(),
        P(None, TENSOR, None),
        P(None, TENSOR),
        P(TENSOR),
        P(TENSOR),
        P(TENSOR, None),
        P(DP + TENSOR, None),
        P(),
        P(DP),
    )
    out_specs = (
        P(DP + TENSOR, None),
        P(DP, TENSOR),
        P(None, TENSOR, None),
        P(TENSOR, None),
        P(None, TENSOR),
        P(TENSOR),
        P(TENSOR),
    )
    return jax.shard_map(
        on_device, mesh=fine, in_specs=in_specs, out_specs=out_specs, check_vma=False
    )
```

```python
import functools

import jax
import jax.numpy as jnp
from jax import lax
from jax.experimental import pallas as pl
from jax.experimental.pallas import tpu as pltpu
from jax.sharding import Mesh
from jax.sharding import PartitionSpec as P

BLK = 8
LANES = 128
EDGE = 16
SIDE = 16
epsilon = 1e-05
MIB = 1024 * 1024

f32 = jnp.float32
bf16 = jnp.bfloat16
SWAP = ((0, 1), (1, 0))
DP = ("zh", "y", "x")
TENSOR = ("zl", "core")


def dot_general(a, b, ca, cb):
    return lax.dot_general(a, b, (((ca,), (cb,)), ((), ())), preferred_element_type=f32)


def full_call(kernel, out_shape, scratch, smem, flops, nbytes, copied=(), sent=(), room=16):
    def call(*args):
        specs = [pl.BlockSpec(memory_space=pltpu.SMEM)] * smem
        specs += [pl.BlockSpec(memory_space=pltpu.VMEM)] * (len(args) - smem)
        for place in copied:
            specs[place] = pl.BlockSpec(memory_space=pl.ANY)
        outs = jax.tree.map(lambda _: pl.BlockSpec(memory_space=pltpu.VMEM), out_shape)
        if sent:
            outs = tuple(
                pl.BlockSpec(memory_space=pl.ANY if k in sent else pltpu.VMEM)
                for k in range(len(out_shape))
            )
        return pl.pallas_call(
            kernel,
            out_shape=out_shape,
            in_specs=specs,
            out_specs=outs,
            scratch_shapes=scratch,
            compiler_params=pltpu.CompilerParams(vmem_limit_bytes=room * MIB),
            cost_estimate=pl.CostEstimate(flops=flops, bytes_accessed=nbytes, transcendentals=0),
        )(*args)

    return call


def outbox_kernel(send, frames_t, out_ref, held):
    part = frames_t.shape[0]
    for c in range(0, part, LANES):
        e = min(part, c + LANES)
        held[:, c:e] = jnp.transpose(frames_t[c:e, :].astype(f32))
    for r in range(out_ref.shape[0]):
        at = pl.ds(pl.multiple_of(send[r] * BLK, BLK), BLK)
        out_ref[r] = held[at, :].astype(bf16)


def pack_kernel(scalars, arrived, rows_out, cols_out, held):
    start, blocks = scalars[0], scalars[1]
    count, _, width = arrived.shape
    for p in range(count):
        block = arrived[lax.rem(start + p, count)].astype(f32)
        held[p * BLK : (p + 1) * BLK, :] = jnp.where(p < blocks, block, 0.0)
    rows = held[...]
    rows_out[...] = rows.astype(bf16)
    for c in range(0, width, LANES):
        e = min(width, c + LANES)
        cols_out[c:e, :] = jnp.transpose(held[:, c:e]).astype(bf16)


def split_rows(unit, cross):
    row = lax.broadcasted_iota(jnp.int32, (SIDE, unit.shape[1]), 0)
    out = jnp.zeros((SIDE, unit.shape[1]), f32)
    for k, value in enumerate((unit, cross)):
        high = value.astype(bf16).astype(f32)
        out = jnp.where(row == 2 * k, high, out)
        out = jnp.where(row == 2 * k + 1, value - high, out)
    return out.astype(bf16)


def main_kernel(
    scalars,
    own_hbm,
    other_hbm,
    gb_ref,
    win_hbm,
    taps_ref,
    scale_ref,
    shift_ref,
    seg_ref,
    delta_hbm,
    wout_hbm,
    x_hbm,
    normed_hbm,
    swish_hbm,
    dlt_hbm,
    keep_hbm,
    send_hbm,
    tap_ref,
    stats_ref,
    glu_s,
    dc_s,
    seg_s,
    w_s,
    bn_s,
    pre_s,
    dglu_s,
    lin_s,
    sig_s,
    tap_s,
    own_ref,
    other_ref,
    win_ref,
    delta_ref,
    wout_ref,
    x_ref,
    normed_ref,
    swish_ref,
    dlt_ref,
    keep_ref,
    send_ref,
    sems,
    out_sems,
):
    def send(k, source, target):
        copy = pltpu.make_async_copy(source, target, out_sems.at[k])
        copy.start()
        sends.append(copy)

    sends = []
    copies = [
        pltpu.make_async_copy(source, target, sems.at[k])
        for k, (source, target) in enumerate(
            (
                (own_hbm, own_ref),
                (other_hbm, other_ref),
                (win_hbm, win_ref),
                (delta_hbm, delta_ref),
                (wout_hbm, wout_ref),
            )
        )
    ]
    for copy in copies:
        copy.start()
    width, slots = x_ref.shape
    part = win_ref.shape[1]
    taps = taps_ref.shape[0]
    rest = part - LANES
    live = scalars[1] * BLK
    core = scalars[3]
    chunk = 64
    steps = width // chunk
    chips = own_ref.shape[0]
    per_part = part // chunk

    w_s[...] = jnp.zeros_like(w_s)
    w_s[0] = taps_ref[:, 0:LANES]
    w_s[1, :, 0:rest] = taps_ref[:, LANES:part]
    bn_s[...] = jnp.zeros_like(bn_s)
    bn_s[0, 0:1, :] = scale_ref[:, 0:LANES]
    bn_s[1, 0:1, 0:rest] = scale_ref[:, LANES:part]
    bn_s[0, 1:2, :] = shift_ref[:, 0:LANES]
    bn_s[1, 1:2, 0:rest] = shift_ref[:, LANES:part]
    seg_s[...] = jnp.full(seg_s.shape, -1, jnp.int32)
    seg_s[EDGE : EDGE + slots, :] = jnp.broadcast_to(seg_ref[...], (slots, LANES))

    glu_s[...] = jnp.zeros_like(glu_s)
    dc_s[...] = jnp.zeros_like(dc_s)
    tap_s[...] = jnp.zeros_like(tap_s)

    copies[0].wait()
    copies[1].wait()

    def fold(v):
        return jnp.sum(v.reshape(chunk // BLK, BLK, slots), axis=0)

    def sum_body(i, acc):
        chip, row = i // per_part, pl.multiple_of(lax.rem(i, per_part) * chunk, chunk)
        for ref, c in ((own_ref, core), (other_ref, 1 - core)):
            value = ref[chip, pl.ds(row, chunk), :]
            to = pl.multiple_of((2 * chip + c) * part + row, chunk)
            x_ref[pl.ds(to, chunk), :] = value
            acc = acc + fold(value.astype(f32))
        return acc

    zero = jnp.zeros((BLK, slots), f32)
    center = lax.fori_loop(0, chips * per_part, sum_body, zero)
    center = jnp.sum(center, axis=0, keepdims=True) / width

    send(0, x_ref, x_hbm)

    def square_body(i, acc):
        return acc + fold(jnp.square(x_ref[pl.ds(i * chunk, chunk), :].astype(f32) - center))

    spread = jnp.sum(lax.fori_loop(0, steps, square_body, zero, unroll=2), axis=0, keepdims=True) / width
    row_scale = lax.rsqrt(spread + epsilon)
    stats_ref[...] = jnp.zeros_like(stats_ref)
    stats_ref[0:1, :] = center
    stats_ref[1:2, :] = row_scale

    def norm_body(i, carry):
        at = pl.ds(i * chunk, chunk)
        standard = (x_ref[at, :].astype(f32) - center) * row_scale
        normed_ref[at, :] = (standard * gb_ref[at, 0:1] + gb_ref[at, 1:2]).astype(bf16)
        return carry

    lax.fori_loop(0, steps, norm_body, 0, unroll=2)

    send(1, normed_ref, normed_hbm)

    copies[2].wait()
    normed = normed_ref[...]
    linear = dot_general(win_ref[0], normed, 1, 0)
    gate_sigmoid = jax.nn.sigmoid(dot_general(win_ref[1], normed, 1, 0))
    lin_s[...] = linear
    sig_s[...] = gate_sigmoid
    is_live = lax.broadcasted_iota(jnp.int32, (part, slots), 1) < live
    glu = jnp.where(is_live, (linear * gate_sigmoid).astype(bf16).astype(f32), 0.0)
    glu_s[0, EDGE : EDGE + slots, :] = jnp.transpose(glu[0:LANES])
    glu_s[1, EDGE : EDGE + slots, 0:rest] = jnp.transpose(glu[LANES:part])

    rows = 64
    blocks = slots // rows

    def conv_body(i, carry):
        base = pl.multiple_of(i * rows, rows)
        here = seg_s[pl.ds(base + EDGE, rows), :]
        acc = [jnp.zeros((rows, LANES), f32) for _ in range(2)]
        for j in range(taps):
            same = seg_s[pl.ds(base + j, rows), :] == here
            for h in range(2):
                value = jnp.where(same, glu_s[h, pl.ds(base + j, rows), :], 0.0)
                acc[h] = acc[h] + value * w_s[h, j : j + 1, :]
        for h in range(2):
            pre_s[h, pl.ds(base, rows), :] = acc[h] * bn_s[h, 0:1, :] + bn_s[h, 1:2, :]
        return carry

    lax.fori_loop(0, blocks, conv_body, 0)

    copies[3].wait()
    copies[4].wait()
    delta_swish = dot_general(delta_ref[...], wout_ref[...], 1, 1)
    row_live = lax.broadcasted_iota(jnp.int32, (slots, LANES), 0) < live
    for h in range(2):
        pre = pre_s[h]
        s = jax.nn.sigmoid(pre)
        swish = jnp.where(row_live, pre * s, 0.0).astype(bf16)
        slope = jnp.where(row_live, s * (1.0 + pre * (1.0 - s)) * bn_s[h, 0:1, :], 0.0)
        if h == 0:
            swish_ref[:, 0:LANES] = swish
            dc_s[h, EDGE : EDGE + slots, :] = delta_swish[:, 0:LANES] * slope
        else:
            swish_ref[:, LANES:part] = swish[:, 0:rest]
            dc_s[h, EDGE : EDGE + slots, 0:rest] = delta_swish[:, LANES:part] * slope[:, 0:rest]

    send(2, swish_ref, swish_hbm)


    def back_body(i, carry):
        base = pl.multiple_of(i * rows, rows)
        here = seg_s[pl.ds(base + EDGE, rows), :]
        alive = (base + lax.broadcasted_iota(jnp.int32, (rows, LANES), 0)) < live
        glu_here = [glu_s[h, pl.ds(base + EDGE, rows), :] for h in range(2)]
        acc = [jnp.zeros((rows, LANES), f32) for _ in range(2)]
        for j in range(taps):
            at = pl.ds(base + (2 * EDGE - j), rows)
            same = seg_s[at, :] == here
            for h in range(2):
                value = jnp.where(same, dc_s[h, at, :], 0.0)
                acc[h] = acc[h] + value * w_s[h, j : j + 1, :]
                tap_s[h, j] += jnp.sum((value * glu_here[h]).reshape(rows // BLK, BLK, LANES), axis=0)
        for h in range(2):
            dglu_s[h, pl.ds(base, rows), :] = jnp.where(alive, acc[h], 0.0)
        return carry

    lax.fori_loop(0, blocks, back_body, 0)
    for h in range(2):
        tap_ref[h] = jnp.sum(tap_s[h], axis=1)

    for h, (c, e) in enumerate(((0, LANES), (LANES, part))):
        dglu = jnp.transpose(dglu_s[h])[0 : e - c]
        s = sig_s[c:e, :]
        dlt_ref[0, c:e, :] = (dglu * s).astype(bf16)
        dlt_ref[1, c:e, :] = (dglu * lin_s[c:e, :] * s * (1.0 - s)).astype(bf16)

    send(3, dlt_ref, dlt_hbm)

    unit = jnp.zeros((BLK, slots), f32)
    cross = jnp.zeros((BLK, slots), f32)
    wide = 2 * part
    for z in range(chips):
        d = z * wide
        term = dot_general(win_ref[0, :, d : d + wide], dlt_ref[0], 0, 0)
        term = term + dot_general(win_ref[1, :, d : d + wide], dlt_ref[1], 0, 0)
        term = term.astype(bf16)
        first, second = term[0:part], term[part:wide]
        keep_ref[z, 0:part, :] = jnp.where(core == 0, first, second)
        send_ref[z, 0:part, :] = jnp.where(core == 0, second, first)
        weighted = term.astype(f32) * gb_ref[d : d + wide, 0:1]
        standard = (x_ref[d : d + wide, :].astype(f32) - center) * row_scale
        unit = unit + jnp.sum(weighted.reshape(wide // BLK, BLK, slots), axis=0)
        cross = cross + jnp.sum((weighted * standard).reshape(wide // BLK, BLK, slots), axis=0)
    totals = split_rows(
        jnp.sum(unit, axis=0, keepdims=True), jnp.sum(cross, axis=0, keepdims=True)
    )
    for z in range(chips):
        send_ref[z, part : part + SIDE, :] = totals
    send(4, send_ref, send_hbm)
    for z in range(chips):
        keep_ref[z, part : part + SIDE, :] = totals
    send(5, keep_ref, keep_hbm)
    for copy in sends:
        copy.wait()


def pair_kernel(scalars, keep_ref, got_ref, *outs):
    chips, rows, _ = keep_ref.shape
    part = rows - SIDE
    side = keep_ref[0, part:rows, :].astype(f32) + got_ref[0, part:rows, :].astype(f32)
    totals = split_rows(side[0:1] + side[1:2], side[2:3] + side[3:4])
    for j in range(chips):
        z = scalars[4] ^ j
        total = keep_ref[z, 0:part, :].astype(f32) + got_ref[z, 0:part, :].astype(f32)
        outs[j][0:part, :] = total.astype(bf16)
        outs[j][part:rows, :] = totals


def sum_kernel(in_ref, out_ref):
    for k in range(out_ref.shape[0]):
        total = sum(in_ref[i, k].astype(f32) for i in range(in_ref.shape[0]))
        out_ref[k] = total.astype(bf16)


def share_kernel(in_ref, home_ref, out_ref):
    peers, _, wide = in_ref.shape
    lines = home_ref.shape[1]
    total = sum(in_ref[i].astype(f32) for i in range(peers)).astype(bf16)
    for i in range(peers):
        out_ref[i, :, 0:wide] = total
        for k in range(lines):
            at = wide + k * 2 * LANES
            out_ref[i, :, at : at + 2 * LANES] = home_ref[i, k]


def unpack_kernel(target, in_ref, weight_ref, out_ref, tap_ref, side_ref, frame_ref, held, turned_rows):
    pieces, _, full = in_ref.shape
    taps, part = tap_ref.shape
    width = weight_ref.shape[1]
    wide = full - 2 * LANES
    extra = wide - width
    per = part // BLK
    left = pieces - 2 * per
    cols = 2 * extra
    for d in range(0, width, cols):
        weight_ref[:, d : d + cols] = in_ref[0 : 2 * per, :, d : d + cols].reshape(2 * part, cols)
        out_ref[0 : left * BLK, d : d + cols] = in_ref[2 * per : pieces, :, d : d + cols].reshape(
            left * BLK, cols
        )
    for c in range(0, width, extra):
        rows = [in_ref[r * (width // extra) + c // extra, :, width:wide] for r in range(per - left)]
        out_ref[left * BLK : part, c : c + extra] = jnp.concatenate(rows, axis=0)
    first = (per - left) * (width // extra)
    for r in range(taps // BLK):
        tap_ref[r * BLK : (r + 1) * BLK, :] = in_ref[first + r, :, width : width + part].astype(f32)
    total = jnp.zeros((BLK, LANES), f32)
    for s in range(pieces):
        held[s] = in_ref[s, :, wide:full].astype(f32)
        total = total + held[s, :, LANES:]
    turned = pltpu.roll(total, LANES - part % LANES, 1)
    low = lax.broadcasted_iota(jnp.int32, (1, LANES), 1) < part % LANES
    for k in range(2):
        side_ref[k : k + 1, 0:LANES] = jnp.where(
            low, turned[3 * k : 3 * k + 1], total[3 * k + 1 : 3 * k + 2]
        )
        side_ref[k : k + 1, LANES:part] = turned[3 * k + 2 : 3 * k + 3, 0 : part - LANES]
    for k in range(frame_ref.shape[1] // BLK):
        turned_rows[k * BLK : (k + 1) * BLK, :] = held[target[k]]
    for c in range(0, part, LANES):
        e = min(part, c + LANES)
        frame_ref[c:e, :] = jnp.transpose(turned_rows[:, c:e]).astype(bf16)


def fan_kernel(in_ref, out_ref):
    lines, peers, _, full = out_ref.shape
    wide = full - 2 * LANES
    for i in range(peers):
        piece = in_ref[i, :, 0:wide]
        for k in range(lines):
            at = wide + k * 2 * LANES
            out_ref[k, i, :, 0:wide] = piece
            out_ref[k, i, :, wide:full] = in_ref[i, :, at : at + 2 * LANES]


def weight_kernel(
    scalars,
    swish_hbm,
    wout_hbm,
    dlt_hbm,
    normed_hbm,
    delta_hbm,
    tap_ref,
    keep_hbm,
    send_hbm,
    grad_hbm,
    swish_ref,
    wout_ref,
    dlt_ref,
    normed_ref,
    delta_ref,
    keep_ref,
    send_ref,
    grad_ref,
    sems,
    out_sems,
):
    inward = (
        (swish_hbm, swish_ref),
        (wout_hbm, wout_ref),
        (dlt_hbm, dlt_ref),
        (normed_hbm, normed_ref),
        (delta_hbm, delta_ref),
    )
    copies = [
        pltpu.make_async_copy(source, target, sems.at[k]) for k, (source, target) in enumerate(inward)
    ]
    for copy in copies:
        copy.start()
    copies[0].wait()
    copies[1].wait()
    width = normed_ref.shape[0]
    part = swish_ref.shape[1]
    taps = tap_ref.shape[1]
    rest = part - LANES
    pieces = grad_ref.shape[0]
    per = part // BLK
    extra = grad_ref.shape[2] - width
    cols = 512
    core = scalars[3]
    chips, half = keep_ref.shape[0:2]
    for z in range(chips):
        at = slice(2 * z * half, 2 * (z + 1) * half)
        term = dot_general(swish_ref[at, :], wout_ref[...], 1, 0).astype(bf16)
        first, second = term[0:half], term[half : 2 * half]
        keep_ref[z] = jnp.where(core == 0, first, second)
        send_ref[z] = jnp.where(core == 0, second, first)
    sends = [
        pltpu.make_async_copy(keep_ref, keep_hbm, out_sems.at[0]),
        pltpu.make_async_copy(send_ref, send_hbm, out_sems.at[1]),
    ]
    for copy in sends:
        copy.start()
    for copy in copies[2:]:
        copy.wait()
    swish_t = jnp.transpose(swish_ref[...].astype(f32)).astype(bf16)
    for d in range(0, width, cols):
        for k in range(2):
            block = dot_general(dlt_ref[k], normed_ref[d : d + cols, :], 1, 1).astype(bf16)
            grad_ref[k * per : (k + 1) * per, :, d : d + cols] = block.reshape(per, BLK, cols)
        block = dot_general(swish_t, delta_ref[:, d : d + cols], 1, 0).astype(bf16)
        left = pieces - 2 * per
        grad_ref[2 * per : pieces, :, d : d + cols] = block[0 : left * BLK].reshape(left, BLK, cols)
        over = block[left * BLK :].reshape(per - left, BLK, cols)
        for r in range(per - left):
            for c in range(0, cols, extra):
                at = r * (width // extra) + (d + c) // extra
                grad_ref[at, :, width : width + extra] = over[r, :, c : c + extra]
    first = (per - left) * (width // extra)
    grad_ref[first:pieces, :, width : width + extra] = jnp.zeros((pieces - first, BLK, extra), bf16)
    for r in range(taps // BLK):
        at = slice(r * BLK, (r + 1) * BLK)
        grad_ref[first + r, :, width : width + LANES] = tap_ref[0, at, :].astype(bf16)
        grad_ref[first + r, :, width + LANES : width + part] = tap_ref[1, at, 0:rest].astype(bf16)
    last = pltpu.make_async_copy(grad_ref, grad_hbm, out_sems.at[2])
    last.start()
    for copy in sends:
        copy.wait()
    last.wait()


def row_kernel(scalars, dn0, dn1, dn2, dn3, x_ref, stats_ref, gain_ref, delta_ref, out_ref, held):
    start, blocks = scalars[0], scalars[1]
    terms = (dn0, dn1, dn2, dn3)
    slots, part = x_ref.shape
    width = scalars[2].astype(f32)
    rest = part - LANES
    count = slots // BLK
    live = blocks * BLK
    totals = sum(term[part : part + SIDE, :].astype(f32) for term in terms)
    unit, cross = totals[0:1] + totals[1:2], totals[2:3] + totals[3:4]
    row = lax.broadcasted_iota(jnp.int32, (BLK, slots), 0)
    side = jnp.where(row == 2, unit, jnp.where(row == 3, cross, stats_ref[...]))
    side = jnp.transpose(side)
    center, row_scale = side[:, 0:1], side[:, 1:2]
    unit, cross = side[:, 2:3] / width, side[:, 3:4] / width
    sums = []
    for h, (c, e) in enumerate(((0, LANES), (LANES, part))):
        dn = jnp.transpose(sum(term[c:e, :].astype(f32) for term in terms))
        standard = (x_ref[:, c:e].astype(f32) - center) * row_scale
        sums.append((jnp.sum(dn * standard, axis=0, keepdims=True), jnp.sum(dn, axis=0, keepdims=True)))
        on = lax.broadcasted_iota(jnp.int32, (slots, e - c), 0) < live
        own = jnp.where(on, delta_ref[:, c:e].astype(f32), 0.0)
        held[h, :, 0 : e - c] = own + row_scale * (dn * gain_ref[:, c:e] - unit - standard * cross)
    held[1, :, rest:LANES] = jnp.zeros((slots, LANES - rest), f32)
    row = lax.broadcasted_iota(jnp.int32, (BLK, LANES), 0)
    lane = lax.broadcasted_iota(jnp.int32, (BLK, LANES), 1)
    beside = jnp.zeros((BLK, LANES), f32)
    for k in range(2):
        low = jnp.broadcast_to(sums[0][k], (BLK, LANES))
        high = jnp.broadcast_to(jnp.concatenate([sums[1][k], sums[1][k]], axis=1), (BLK, LANES))
        beside = jnp.where(row == 3 * k, pltpu.roll(low, 64, 1), beside)
        beside = jnp.where(row == 3 * k + 1, low, beside)
        beside = jnp.where(row == 3 * k + 2, high, beside)
    for s in range(count):
        at = pl.ds(pl.multiple_of(lax.rem(s - start + 16 * count, count) * BLK, BLK), BLK)
        out_ref[s, :, 0:LANES] = held[0, at, :].astype(bf16)
        out_ref[s, :, LANES : 2 * LANES] = jnp.where(lane < rest, held[1, at, :], beside).astype(bf16)


def on_device(
    frames,
    norm_gain,
    norm_bias,
    input_weight,
    depth_weight,
    batch_scale,
    batch_shift,
    output_weight,
    upstream,
    replica_blocks,
    segment,
):
    replicas = lax.axis_size(DP)
    my_index = lax.axis_index(DP)
    tensor_index = lax.axis_index(TENSOR)
    width = norm_gain.shape[0]
    load_rows, part = frames.shape
    slots = segment.shape[0]
    rows_part = upstream.shape[0]
    taps = depth_weight.shape[0]
    load_blocks = load_rows // BLK
    count = slots // BLK

    delta = lax.all_gather(upstream, TENSOR, axis=0, tiled=True)

    ends = jnp.cumsum(replica_blocks)
    starts = ends - replica_blocks
    send = jnp.clip((starts - my_index + replicas - 1) // replicas, 0, load_blocks - 1)
    numbers = my_index + replicas * jnp.arange(load_blocks, dtype=jnp.int32)
    target = jnp.sum((ends[None, :] <= numbers[:, None]).astype(jnp.int32), axis=1)
    is_mine = jnp.arange(replicas, dtype=jnp.int32) == my_index
    my_start = jnp.sum(jnp.where(is_mine, starts, 0))
    my_blocks = jnp.sum(jnp.where(is_mine, replica_blocks, 0))
    core = lax.axis_index("core")
    scalars = jnp.stack([lax.rem(my_start, replicas), my_blocks, jnp.int32(width), core, lax.axis_index("zl")])

    sds = jax.ShapeDtypeStruct
    outbox = full_call(
        outbox_kernel,
        sds((replicas, BLK, part), bf16),
        [pltpu.VMEM((load_rows, part), f32)],
        1,
        1000,
        400000,
    )(send, frames.T)
    arrived = lax.all_to_all(outbox, DP, split_axis=0, concat_axis=0, tiled=True)

    both = jnp.stack([norm_gain, norm_bias], axis=1)
    arrived, both, seg_column = lax.optimization_barrier((arrived, both, segment[:, None]))
    packed, packed_t = full_call(
        pack_kernel,
        (sds((slots, part), bf16), sds((part, slots), bf16)),
        [pltpu.VMEM((slots, part), f32)],
        1,
        1000,
        1000000,
    )(scalars, arrived)
    own = lax.all_gather(packed_t, "zl", axis=0)
    other = lax.ppermute(own, "core", SWAP)
    chips = own.shape[0]

    gathered, normed, swish, dlt, keep, send_half, tap, stats = full_call(
        main_kernel,
        (
            sds((width, slots), bf16),
            sds((width, slots), bf16),
            sds((slots, part), bf16),
            sds((2, part, slots), bf16),
            sds((chips, part + SIDE, slots), bf16),
            sds((chips, part + SIDE, slots), bf16),
            sds((2, taps, LANES), f32),
            sds((BLK, slots), f32),
        ),
        [
            pltpu.VMEM((2, slots + 2 * EDGE, LANES), f32),
            pltpu.VMEM((2, slots + 2 * EDGE, LANES), f32),
            pltpu.VMEM((slots + 2 * EDGE, LANES), jnp.int32),
            pltpu.VMEM((2, taps, LANES), f32),
            pltpu.VMEM((2, BLK, LANES), f32),
            pltpu.VMEM((2, slots, LANES), f32),
            pltpu.VMEM((2, slots, LANES), f32),
            pltpu.VMEM((part, slots), f32),
            pltpu.VMEM((part, slots), f32),
            pltpu.VMEM((2, taps, BLK, LANES), f32),
            pltpu.VMEM(own.shape, bf16),
            pltpu.VMEM(other.shape, bf16),
            pltpu.VMEM(input_weight.shape, bf16),
            pltpu.VMEM(delta.shape, bf16),
            pltpu.VMEM(output_weight.shape, bf16),
            pltpu.VMEM((width, slots), bf16),
            pltpu.VMEM((width, slots), bf16),
            pltpu.VMEM((slots, part), bf16),
            pltpu.VMEM((2, part, slots), bf16),
            pltpu.VMEM((chips, part + SIDE, slots), bf16),
            pltpu.VMEM((chips, part + SIDE, slots), bf16),
            pltpu.SemaphoreType.DMA((5,)),
            pltpu.SemaphoreType.DMA((6,)),
        ],
        1,
        2000000000,
        10000000,
        (1, 2, 4, 9, 10),
        (0, 1, 2, 3, 4, 5),
        60,
    )(
        scalars,
        own,
        other,
        both,
        input_weight,
        depth_weight,
        batch_scale[None],
        batch_shift[None],
        seg_column,
        delta,
        output_weight,
    )
    got = lax.ppermute(send_half, "core", SWAP)
    paired = full_call(
        pair_kernel, (sds(keep.shape[1:], bf16),) * chips, [], 1, 1000000, 2400000
    )(scalars, keep, got)
    terms = [paired[0]] + [
        lax.ppermute(paired[j], "zl", [(z, z ^ j) for z in range(chips)]) for j in range(1, chips)
    ]

    pieces = replicas
    mixed_keep, mixed_send, grads = full_call(
        weight_kernel,
        (
            sds((chips, rows_part, width), bf16),
            sds((chips, rows_part, width), bf16),
            sds((pieces, BLK, width + 2 * LANES), bf16),
        ),
        [
            pltpu.VMEM(swish.shape, bf16),
            pltpu.VMEM(output_weight.shape, bf16),
            pltpu.VMEM(dlt.shape, bf16),
            pltpu.VMEM(normed.shape, bf16),
            pltpu.VMEM(delta.shape, bf16),
            pltpu.VMEM((chips, rows_part, width), bf16),
            pltpu.VMEM((chips, rows_part, width), bf16),
            pltpu.VMEM((pieces, BLK, width + 2 * LANES), bf16),
            pltpu.SemaphoreType.DMA((5,)),
            pltpu.SemaphoreType.DMA((3,)),
        ],
        1,
        1500000000,
        8000000,
        (1, 2, 3, 4, 5),
        (0, 1, 2),
        60,
    )(scalars, swish, output_weight, dlt, normed, delta, tap)
    lines, peers = lax.axis_size("x"), lax.axis_size(("zh", "y"))
    grads, _ = lax.optimization_barrier((grads, paired[0]))
    grads = grads.reshape((lines, peers) + grads.shape[1:])
    grads = lax.all_to_all(grads, "x", split_axis=0, concat_axis=0, tiled=True)
    grads, *terms = lax.optimization_barrier((grads, *terms))
    grads = full_call(sum_kernel, sds(grads.shape[1:], bf16), [], 0, 1000000, 2300000)(grads)
    grads = lax.all_to_all(grads, ("zh", "y"), split_axis=0, concat_axis=0, tiled=True)

    mixed = mixed_keep.astype(f32) + lax.ppermute(mixed_send, "core", SWAP).astype(f32)
    mixed = mixed.astype(bf16).reshape(chips * rows_part, width)
    mixed, *terms = lax.optimization_barrier((mixed, *terms))
    mixed_sum = lax.psum_scatter(mixed, "zl", scatter_dimension=0, tiled=True)

    column_start = tensor_index * part
    gain_part = lax.dynamic_slice_in_dim(norm_gain, column_start, part)[None]
    delta_part = lax.dynamic_slice_in_dim(delta, column_start, part, 1)
    homebound = full_call(
        row_kernel,
        sds((count, BLK, 2 * LANES), bf16),
        [pltpu.VMEM((2, slots, LANES), f32)],
        1,
        1000000,
        1000000,
    )(scalars, *terms, packed, stats, gain_part, delta_part)
    wide = grads.shape[-1]
    shared = full_call(
        share_kernel, sds((peers, BLK, wide + lines * 2 * LANES), bf16), [], 0, 1000000, 1500000
    )(grads, homebound.reshape(peers, lines, BLK, 2 * LANES))
    shared = lax.all_to_all(shared, ("zh", "y"), split_axis=0, concat_axis=0, tiled=True)
    fanned = full_call(
        fan_kernel, sds((lines, peers, BLK, wide + 2 * LANES), bf16), [], 0, 1000000, 3000000
    )(shared)
    whole = lax.all_to_all(fanned, "x", split_axis=0, concat_axis=0, tiled=True)
    whole = whole.reshape((pieces,) + whole.shape[2:])
    target = lax.rem(target, lines) * peers + target // lines
    weight_grad, out_grad, tap_grad, side, frame_gradient = full_call(
        unpack_kernel,
        (
            sds((2 * part, width), bf16),
            sds((part, width), bf16),
            sds((taps, part), f32),
            sds((2, part), f32),
            sds((part, load_rows), bf16),
        ),
        [pltpu.VMEM((pieces, BLK, 2 * LANES), f32), pltpu.VMEM((load_rows, 2 * LANES), f32)],
        1,
        1000000,
        5000000,
    )(target, whole)
    weight_grad = weight_grad.reshape(2, part, width)
    frame_gradient = frame_gradient.T

    row_start = tensor_index * rows_part
    live_mine = (row_start + jnp.arange(rows_part, dtype=jnp.int32) < my_blocks * BLK)[:, None]
    residual = lax.dynamic_slice_in_dim(gathered, row_start, rows_part, 1).T
    block_output = jnp.where(
        live_mine, residual.astype(f32) + mixed_sum.astype(f32), 0.0
    ).astype(bf16)
    return (block_output, frame_gradient, weight_grad, out_grad, tap_grad, side[0], side[1])


def solution(mesh):
    fine = Mesh(mesh.devices.reshape(2, 8, 4, 4, 2), DP + TENSOR)
    in_specs = (
        P(DP, TENSOR),
        P(),
        P(),
        P(None, TENSOR, None),
        P(None, TENSOR),
        P(TENSOR),
        P(TENSOR),
        P(TENSOR, None),
        P(DP + TENSOR, None),
        P(),
        P(DP),
    )
    out_specs = (
        P(DP + TENSOR, None),
        P(DP, TENSOR),
        P(None, TENSOR, None),
        P(TENSOR, None),
        P(None, TENSOR),
        P(TENSOR),
        P(TENSOR),
    )
    return jax.shard_map(
        on_device, mesh=fine, in_specs=in_specs, out_specs=out_specs, check_vma=False
    )
```

```python
import functools

import jax
import jax.numpy as jnp
from jax import lax
from jax.experimental import pallas as pl
from jax.experimental.pallas import tpu as pltpu
from jax.sharding import Mesh
from jax.sharding import PartitionSpec as P

BLK = 8
LANES = 128
EDGE = 16
SIDE = 16
epsilon = 1e-05
MIB = 1024 * 1024

f32 = jnp.float32
bf16 = jnp.bfloat16
SWAP = ((0, 1), (1, 0))
DP = ("zh", "y", "x")
TENSOR = ("zl", "core")


def dot_general(a, b, ca, cb):
    return lax.dot_general(a, b, (((ca,), (cb,)), ((), ())), preferred_element_type=f32)


def full_call(kernel, out_shape, scratch, smem, flops, nbytes, copied=(), sent=(), room=16):
    def call(*args):
        specs = [pl.BlockSpec(memory_space=pltpu.SMEM)] * smem
        specs += [pl.BlockSpec(memory_space=pltpu.VMEM)] * (len(args) - smem)
        for place in copied:
            specs[place] = pl.BlockSpec(memory_space=pl.ANY)
        outs = jax.tree.map(lambda _: pl.BlockSpec(memory_space=pltpu.VMEM), out_shape)
        if sent:
            outs = tuple(
                pl.BlockSpec(memory_space=pl.ANY if k in sent else pltpu.VMEM)
                for k in range(len(out_shape))
            )
        return pl.pallas_call(
            kernel,
            out_shape=out_shape,
            in_specs=specs,
            out_specs=outs,
            scratch_shapes=scratch,
            compiler_params=pltpu.CompilerParams(vmem_limit_bytes=room * MIB),
            cost_estimate=pl.CostEstimate(flops=flops, bytes_accessed=nbytes, transcendentals=0),
        )(*args)

    return call


def outbox_kernel(replica_blocks, place, frames_hbm, out_ref, held, frames_t, sem):
    copy = pltpu.make_async_copy(frames_hbm, frames_t, sem)
    copy.start()
    part, rows = frames_t.shape
    count = out_ref.shape[0]
    copy.wait()
    for c in range(0, part, LANES):
        e = min(part, c + LANES)
        held[:, c:e] = jnp.transpose(frames_t[c:e, :].astype(f32))
    start = jnp.int32(0)
    for r in range(count):
        block = jnp.minimum(lax.div(start - place[0] + (count - 1), count), rows // BLK - 1)
        at = pl.ds(pl.multiple_of(block * BLK, BLK), BLK)
        out_ref[r] = held[at, :].astype(bf16)
        start = start + replica_blocks[r]


def pack_kernel(scalars, arrived, rows_out, cols_out, held):
    start, blocks = scalars[0], scalars[1]
    count, _, width = arrived.shape
    for p in range(count):
        block = arrived[lax.rem(start + p, count)].astype(f32)
        held[p * BLK : (p + 1) * BLK, :] = jnp.where(p < blocks, block, 0.0)
    rows = held[...]
    rows_out[...] = rows.astype(bf16)
    for c in range(0, width, LANES):
        e = min(width, c + LANES)
        cols_out[c:e, :] = jnp.transpose(held[:, c:e]).astype(bf16)


def split_rows(unit, cross):
    row = lax.broadcasted_iota(jnp.int32, (SIDE, unit.shape[1]), 0)
    out = jnp.zeros((SIDE, unit.shape[1]), f32)
    for k, value in enumerate((unit, cross)):
        high = value.astype(bf16).astype(f32)
        out = jnp.where(row == 2 * k, high, out)
        out = jnp.where(row == 2 * k + 1, value - high, out)
    return out.astype(bf16)


def main_kernel(
    scalars,
    own_hbm,
    other_hbm,
    gain_ref,
    bias_ref,
    win_hbm,
    taps_ref,
    scale_ref,
    shift_ref,
    seg_ref,
    delta_hbm,
    wout_hbm,
    x_hbm,
    keep_hbm,
    send_hbm,
    mixed_keep_hbm,
    mixed_send_hbm,
    grad_hbm,
    stats_ref,
    gb_ref,
    dsw_s,
    mixed_s,
    grad_ref,
    glu_s,
    dc_s,
    seg_s,
    w_s,
    bn_s,
    pre_s,
    dglu_s,
    lin_s,
    sig_s,
    tap_s,
    own_ref,
    other_ref,
    win_ref,
    delta_ref,
    wout_ref,
    x_ref,
    normed_ref,
    swish_ref,
    dlt_ref,
    keep_ref,
    send_ref,
    sems,
    out_sems,
):
    def send(k, source, target):
        copy = pltpu.make_async_copy(source, target, out_sems.at[k])
        copy.start()
        sends.append(copy)

    sends = []
    copies = [
        pltpu.make_async_copy(source, target, sems.at[k])
        for k, (source, target) in enumerate(
            (
                (own_hbm, own_ref),
                (other_hbm, other_ref),
                (win_hbm, win_ref),
                (delta_hbm, delta_ref),
                (wout_hbm, wout_ref),
            )
        )
    ]
    for copy in copies:
        copy.start()
    width, slots = x_ref.shape
    part = win_ref.shape[1]
    taps = taps_ref.shape[0]
    rest = part - LANES
    live = scalars[1] * BLK
    core = scalars[3]
    chunk = 64
    steps = width // chunk
    chips = own_ref.shape[0]
    per_part = part // chunk

    w_s[...] = jnp.zeros_like(w_s)
    w_s[0] = taps_ref[:, 0:LANES]
    w_s[1, :, 0:rest] = taps_ref[:, LANES:part]
    bn_s[...] = jnp.zeros_like(bn_s)
    bn_s[0, 0:1, :] = scale_ref[:, 0:LANES]
    bn_s[1, 0:1, 0:rest] = scale_ref[:, LANES:part]
    bn_s[0, 1:2, :] = shift_ref[:, 0:LANES]
    bn_s[1, 1:2, 0:rest] = shift_ref[:, LANES:part]
    row = lax.broadcasted_iota(jnp.int32, (BLK, width), 0)
    gb_ref[...] = jnp.transpose(jnp.where(row == 0, gain_ref[...], bias_ref[...]))
    segments = jnp.broadcast_to(seg_ref[...].astype(f32), (BLK, slots))
    seg_s[...] = jnp.full(seg_s.shape, -1.0, f32)
    seg_s[EDGE : EDGE + slots, :] = jnp.broadcast_to(jnp.transpose(segments)[:, 0:1], (slots, LANES))

    glu_s[...] = jnp.zeros_like(glu_s)
    dc_s[...] = jnp.zeros_like(dc_s)
    tap_s[...] = jnp.zeros_like(tap_s)

    copies[0].wait()
    copies[1].wait()

    def fold(v):
        return jnp.sum(v.reshape(chunk // BLK, BLK, slots), axis=0)

    def sum_body(i, acc):
        chip, row = i // per_part, pl.multiple_of(lax.rem(i, per_part) * chunk, chunk)
        for ref, c in ((own_ref, core), (other_ref, 1 - core)):
            value = ref[chip, pl.ds(row, chunk), :]
            to = pl.multiple_of((2 * chip + c) * part + row, chunk)
            x_ref[pl.ds(to, chunk), :] = value
            acc = acc + fold(value.astype(f32))
        return acc

    zero = jnp.zeros((BLK, slots), f32)
    center = lax.fori_loop(0, chips * per_part, sum_body, zero)
    center = jnp.sum(center, axis=0, keepdims=True) / width

    send(0, x_ref, x_hbm)

    def square_body(i, acc):
        return acc + fold(jnp.square(x_ref[pl.ds(i * chunk, chunk), :].astype(f32) - center))

    spread = jnp.sum(lax.fori_loop(0, steps, square_body, zero, unroll=2), axis=0, keepdims=True) / width
    row_scale = lax.rsqrt(spread + epsilon)
    stats_ref[...] = jnp.zeros_like(stats_ref)
    stats_ref[0:1, :] = center
    stats_ref[1:2, :] = row_scale

    def norm_body(i, carry):
        at = pl.ds(i * chunk, chunk)
        standard = (x_ref[at, :].astype(f32) - center) * row_scale
        normed_ref[at, :] = (standard * gb_ref[at, 0:1] + gb_ref[at, 1:2]).astype(bf16)
        return carry

    lax.fori_loop(0, steps, norm_body, 0, unroll=2)


    copies[2].wait()
    normed = normed_ref[...]
    linear = dot_general(win_ref[0], normed, 1, 0)
    gate_sigmoid = jax.nn.sigmoid(dot_general(win_ref[1], normed, 1, 0))
    lin_s[...] = linear
    sig_s[...] = gate_sigmoid
    is_live = lax.broadcasted_iota(jnp.int32, (part, slots), 1) < live
    glu = jnp.where(is_live, (linear * gate_sigmoid).astype(bf16).astype(f32), 0.0)
    glu_s[0, EDGE : EDGE + slots, :] = jnp.transpose(glu[0:LANES])
    glu_s[1, EDGE : EDGE + slots, 0:rest] = jnp.transpose(glu[LANES:part])

    rows = 64
    blocks = slots // rows
    copies[3].wait()
    copies[4].wait()

    def conv_body(i, carry):
        base = pl.multiple_of(i * rows, rows)
        dsw_s[pl.ds(base, rows), :] = dot_general(delta_ref[pl.ds(base, rows), :], wout_ref[...], 1, 1)
        here = seg_s[pl.ds(base + EDGE, rows), :]
        acc = [jnp.zeros((rows, LANES), f32) for _ in range(2)]
        for j in range(taps):
            same = seg_s[pl.ds(base + j, rows), :] == here
            for h in range(2):
                value = jnp.where(same, glu_s[h, pl.ds(base + j, rows), :], 0.0)
                acc[h] = acc[h] + value * w_s[h, j : j + 1, :]
        for h in range(2):
            pre_s[h, pl.ds(base, rows), :] = acc[h] * bn_s[h, 0:1, :] + bn_s[h, 1:2, :]
        return carry

    lax.fori_loop(0, blocks, conv_body, 0)

    delta_swish = dsw_s[...]
    row_live = lax.broadcasted_iota(jnp.int32, (slots, LANES), 0) < live
    for h in range(2):
        pre = pre_s[h]
        s = jax.nn.sigmoid(pre)
        swish = jnp.where(row_live, pre * s, 0.0).astype(bf16)
        slope = jnp.where(row_live, s * (1.0 + pre * (1.0 - s)) * bn_s[h, 0:1, :], 0.0)
        if h == 0:
            swish_ref[:, 0:LANES] = swish
            dc_s[h, EDGE : EDGE + slots, :] = delta_swish[:, 0:LANES] * slope
        else:
            swish_ref[:, LANES:part] = swish[:, 0:rest]
            dc_s[h, EDGE : EDGE + slots, 0:rest] = delta_swish[:, LANES:part] * slope[:, 0:rest]

    swish_t = jnp.transpose(swish_ref[...].astype(f32)).astype(bf16)


    def back_body(i, carry):
        base = pl.multiple_of(i * rows, rows)
        mixed = dot_general(swish_ref[pl.ds(base, rows), :], wout_ref[...], 1, 0)
        mixed_s[lax.rem(i, 2) ^ core, i // 2] = mixed.astype(bf16)
        here = seg_s[pl.ds(base + EDGE, rows), :]
        alive = (base + lax.broadcasted_iota(jnp.int32, (rows, LANES), 0)) < live
        glu_here = [glu_s[h, pl.ds(base + EDGE, rows), :] for h in range(2)]
        acc = [jnp.zeros((rows, LANES), f32) for _ in range(2)]
        for j in range(taps):
            at = pl.ds(base + (2 * EDGE - j), rows)
            same = seg_s[at, :] == here
            for h in range(2):
                value = jnp.where(same, dc_s[h, at, :], 0.0)
                acc[h] = acc[h] + value * w_s[h, j : j + 1, :]
                tap_s[h, j] += jnp.sum((value * glu_here[h]).reshape(rows // BLK, BLK, LANES), axis=0)
        for h in range(2):
            dglu_s[h, pl.ds(base, rows), :] = jnp.where(alive, acc[h], 0.0)
        return carry

    lax.fori_loop(0, blocks, back_body, 0)
    send(1, mixed_s.at[0], mixed_keep_hbm)
    send(2, mixed_s.at[1], mixed_send_hbm)

    per = part // BLK
    parts = grad_ref.shape[0]
    extra = grad_ref.shape[2] - width
    left = parts - 2 * per
    cols = 512
    for d in range(0, width, cols):
        block = dot_general(swish_t, delta_ref[:, d : d + cols], 1, 0).astype(bf16)
        grad_ref[2 * per : parts, :, d : d + cols] = block[0 : left * BLK].reshape(left, BLK, cols)
        over = block[left * BLK :].reshape(per - left, BLK, cols)
        for r in range(per - left):
            for c in range(0, cols, extra):
                at = r * (width // extra) + (d + c) // extra
                grad_ref[at, :, width : width + extra] = over[r, :, c : c + extra]
    first = (per - left) * (width // extra)
    grad_ref[first:parts, :, width : width + extra] = jnp.zeros((parts - first, BLK, extra), bf16)
    for h, (c, e) in enumerate(((0, LANES), (LANES, part))):
        tap = jnp.sum(tap_s[h], axis=1)[:, 0 : e - c].astype(bf16)
        for r in range(taps // BLK):
            grad_ref[first + r, :, width + c : width + e] = tap[r * BLK : (r + 1) * BLK]

    def depart(k, begin, end):
        send(k, grad_ref.at[begin:end], grad_hbm.at[begin:end])

    depart(3, 2 * per, parts)

    for h, (c, e) in enumerate(((0, LANES), (LANES, part))):
        dglu = jnp.transpose(dglu_s[h])[0 : e - c]
        s = sig_s[c:e, :]
        dlt_ref[0, c:e, :] = (dglu * s).astype(bf16)
        dlt_ref[1, c:e, :] = (dglu * lin_s[c:e, :] * s * (1.0 - s)).astype(bf16)


    unit = jnp.zeros((BLK, slots), f32)
    cross = jnp.zeros((BLK, slots), f32)
    wide = 2 * part
    for z in range(chips):
        d = z * wide
        term = dot_general(win_ref[0, :, d : d + wide], dlt_ref[0], 0, 0)
        term = term + dot_general(win_ref[1, :, d : d + wide], dlt_ref[1], 0, 0)
        term = term.astype(bf16)
        first, second = term[0:part], term[part:wide]
        send_ref[z, 0:part, :] = jnp.where(core == 0, second, first)
        send(6 + z, send_ref.at[z, 0:part], send_hbm.at[z, 0:part])
        keep_ref[z, 0:part, :] = jnp.where(core == 0, first, second)
        send(6 + chips + z, keep_ref.at[z, 0:part], keep_hbm.at[z, 0:part])
        weighted = term.astype(f32) * gb_ref[d : d + wide, 0:1]
        standard = (x_ref[d : d + wide, :].astype(f32) - center) * row_scale
        unit = unit + jnp.sum(weighted.reshape(wide // BLK, BLK, slots), axis=0)
        cross = cross + jnp.sum((weighted * standard).reshape(wide // BLK, BLK, slots), axis=0)
    totals = split_rows(
        jnp.sum(unit, axis=0, keepdims=True), jnp.sum(cross, axis=0, keepdims=True)
    )
    for z in range(chips):
        send_ref[z, part : part + SIDE, :] = totals
        keep_ref[z, part : part + SIDE, :] = totals
    below = pl.ds(part, SIDE)
    send(6 + 2 * chips, send_ref.at[:, below], send_hbm.at[:, below])
    send(7 + 2 * chips, keep_ref.at[:, below], keep_hbm.at[:, below])

    for k in range(2):
        for d in range(0, width, cols):
            block = dot_general(dlt_ref[k], normed_ref[d : d + cols, :], 1, 1).astype(bf16)
            grad_ref[k * per : (k + 1) * per, :, d : d + cols] = block.reshape(per, BLK, cols)
        depart(4 + k, k * per, (k + 1) * per)
    for copy in sends:
        copy.wait()


def pair_kernel(scalars, keep_ref, got_ref, *outs):
    chips, rows, _ = keep_ref.shape
    part = rows - SIDE
    side = keep_ref[0, part:rows, :].astype(f32) + got_ref[0, part:rows, :].astype(f32)
    totals = split_rows(side[0:1] + side[1:2], side[2:3] + side[3:4])
    for j in range(chips):
        z = scalars[4] ^ j
        total = keep_ref[z, 0:part, :].astype(f32) + got_ref[z, 0:part, :].astype(f32)
        outs[j][0:part, :] = total.astype(bf16)
        outs[j][part:rows, :] = totals


def sum_kernel(in_ref, out_ref):
    for k in range(out_ref.shape[0]):
        total = sum(in_ref[i, k].astype(f32) for i in range(in_ref.shape[0]))
        out_ref[k] = total.astype(bf16)


def share_kernel(in_ref, home_ref, out_ref):
    peers, _, wide = in_ref.shape
    lines = home_ref.shape[1]
    total = sum(in_ref[i].astype(f32) for i in range(peers)).astype(bf16)
    for i in range(peers):
        out_ref[i, :, 0:wide] = total
        for k in range(lines):
            at = wide + k * 2 * LANES
            out_ref[i, :, at : at + 2 * LANES] = home_ref[i, k]


def unpack_kernel(target, in_ref, weight_ref, out_ref, tap_ref, side_ref, frame_ref, held, turned_rows):
    pieces, _, full = in_ref.shape
    taps, part = tap_ref.shape
    width = weight_ref.shape[1]
    wide = full - 2 * LANES
    extra = wide - width
    per = part // BLK
    left = pieces - 2 * per
    cols = 2 * extra
    for d in range(0, width, cols):
        weight_ref[:, d : d + cols] = in_ref[0 : 2 * per, :, d : d + cols].reshape(2 * part, cols)
        out_ref[0 : left * BLK, d : d + cols] = in_ref[2 * per : pieces, :, d : d + cols].reshape(
            left * BLK, cols
        )
    for c in range(0, width, extra):
        rows = [in_ref[r * (width // extra) + c // extra, :, width:wide] for r in range(per - left)]
        out_ref[left * BLK : part, c : c + extra] = jnp.concatenate(rows, axis=0)
    first = (per - left) * (width // extra)
    for r in range(taps // BLK):
        tap_ref[r * BLK : (r + 1) * BLK, :] = in_ref[first + r, :, width : width + part].astype(f32)
    total = jnp.zeros((BLK, LANES), f32)
    for s in range(pieces):
        held[s] = in_ref[s, :, wide:full].astype(f32)
        total = total + held[s, :, LANES:]
    turned = pltpu.roll(total, LANES - part % LANES, 1)
    low = lax.broadcasted_iota(jnp.int32, (1, LANES), 1) < part % LANES
    for k in range(2):
        side_ref[k : k + 1, 0:LANES] = jnp.where(
            low, turned[3 * k : 3 * k + 1], total[3 * k + 1 : 3 * k + 2]
        )
        side_ref[k : k + 1, LANES:part] = turned[3 * k + 2 : 3 * k + 3, 0 : part - LANES]
    for k in range(frame_ref.shape[1] // BLK):
        turned_rows[k * BLK : (k + 1) * BLK, :] = held[target[k]]
    for c in range(0, part, LANES):
        e = min(part, c + LANES)
        frame_ref[c:e, :] = jnp.transpose(turned_rows[:, c:e]).astype(bf16)


def fan_kernel(in_ref, out_ref):
    lines, peers, _, full = out_ref.shape
    wide = full - 2 * LANES
    for i in range(peers):
        piece = in_ref[i, :, 0:wide]
        for k in range(lines):
            at = wide + k * 2 * LANES
            out_ref[k, i, :, 0:wide] = piece
            out_ref[k, i, :, wide:full] = in_ref[i, :, at : at + 2 * LANES]


def row_kernel(scalars, dn0, dn1, dn2, dn3, x_ref, stats_ref, gain_ref, delta_ref, out_ref, held):
    start, blocks = scalars[0], scalars[1]
    terms = (dn0, dn1, dn2, dn3)
    slots, part = x_ref.shape
    width = scalars[2].astype(f32)
    rest = part - LANES
    count = slots // BLK
    live = blocks * BLK
    totals = sum(term[part : part + SIDE, :].astype(f32) for term in terms)
    unit, cross = totals[0:1] + totals[1:2], totals[2:3] + totals[3:4]
    row = lax.broadcasted_iota(jnp.int32, (BLK, slots), 0)
    side = jnp.where(row == 2, unit, jnp.where(row == 3, cross, stats_ref[...]))
    side = jnp.transpose(side)
    center, row_scale = side[:, 0:1], side[:, 1:2]
    unit, cross = side[:, 2:3] / width, side[:, 3:4] / width
    sums = []
    for h, (c, e) in enumerate(((0, LANES), (LANES, part))):
        dn = jnp.transpose(sum(term[c:e, :].astype(f32) for term in terms))
        standard = (x_ref[:, c:e].astype(f32) - center) * row_scale
        sums.append((jnp.sum(dn * standard, axis=0, keepdims=True), jnp.sum(dn, axis=0, keepdims=True)))
        on = lax.broadcasted_iota(jnp.int32, (slots, e - c), 0) < live
        own = jnp.where(on, delta_ref[:, c:e].astype(f32), 0.0)
        held[h, :, 0 : e - c] = own + row_scale * (dn * gain_ref[:, c:e] - unit - standard * cross)
    held[1, :, rest:LANES] = jnp.zeros((slots, LANES - rest), f32)
    row = lax.broadcasted_iota(jnp.int32, (BLK, LANES), 0)
    lane = lax.broadcasted_iota(jnp.int32, (BLK, LANES), 1)
    beside = jnp.zeros((BLK, LANES), f32)
    for k in range(2):
        low = jnp.broadcast_to(sums[0][k], (BLK, LANES))
        high = jnp.broadcast_to(jnp.concatenate([sums[1][k], sums[1][k]], axis=1), (BLK, LANES))
        beside = jnp.where(row == 3 * k, pltpu.roll(low, 64, 1), beside)
        beside = jnp.where(row == 3 * k + 1, low, beside)
        beside = jnp.where(row == 3 * k + 2, high, beside)
    for s in range(count):
        at = pl.ds(pl.multiple_of(lax.rem(s - start + 16 * count, count) * BLK, BLK), BLK)
        out_ref[s, :, 0:LANES] = held[0, at, :].astype(bf16)
        out_ref[s, :, LANES : 2 * LANES] = jnp.where(lane < rest, held[1, at, :], beside).astype(bf16)


def on_device(
    frames,
    norm_gain,
    norm_bias,
    input_weight,
    depth_weight,
    batch_scale,
    batch_shift,
    output_weight,
    upstream,
    replica_blocks,
    segment,
):
    replicas = lax.axis_size(DP)
    my_index = lax.axis_index(DP)
    tensor_index = lax.axis_index(TENSOR)
    width = norm_gain.shape[0]
    load_rows, part = frames.shape
    slots = segment.shape[0]
    rows_part = upstream.shape[0]
    taps = depth_weight.shape[0]
    load_blocks = load_rows // BLK
    count = slots // BLK

    delta = lax.all_gather(upstream, TENSOR, axis=0, tiled=True)

    ends = jnp.cumsum(replica_blocks)
    starts = ends - replica_blocks
    numbers = my_index + replicas * jnp.arange(load_blocks, dtype=jnp.int32)
    target = jnp.sum((ends[None, :] <= numbers[:, None]).astype(jnp.int32), axis=1)
    is_mine = jnp.arange(replicas, dtype=jnp.int32) == my_index
    my_start = jnp.sum(jnp.where(is_mine, starts, 0))
    my_blocks = jnp.sum(jnp.where(is_mine, replica_blocks, 0))
    core = lax.axis_index("core")
    scalars = jnp.stack([lax.rem(my_start, replicas), my_blocks, jnp.int32(width), core, lax.axis_index("zl")])

    sds = jax.ShapeDtypeStruct
    outbox = full_call(
        outbox_kernel,
        sds((replicas, BLK, part), bf16),
        [
            pltpu.VMEM((load_rows, part), f32),
            pltpu.VMEM((part, load_rows), bf16),
            pltpu.SemaphoreType.DMA(()),
        ],
        2,
        1000,
        400000,
        (2,),
    )(replica_blocks, my_index[None], frames.T)
    arrived = lax.all_to_all(outbox, DP, split_axis=0, concat_axis=0, tiled=True)

    packed, packed_t = full_call(
        pack_kernel,
        (sds((slots, part), bf16), sds((part, slots), bf16)),
        [pltpu.VMEM((slots, part), f32)],
        1,
        1000,
        1000000,
    )(scalars, arrived)
    own = lax.all_gather(packed_t, "zl", axis=0)
    other = lax.ppermute(own, "core", SWAP)
    chips = own.shape[0]

    pieces = replicas
    half = sds((chips, rows_part, width), bf16)
    gathered, keep, send_half, mixed_keep, mixed_send, grads, stats = full_call(
        main_kernel,
        (
            sds((width, slots), bf16),
            sds((chips, part + SIDE, slots), bf16),
            sds((chips, part + SIDE, slots), bf16),
            half,
            half,
            sds((pieces, BLK, width + 2 * LANES), bf16),
            sds((BLK, slots), f32),
        ),
        [
            pltpu.VMEM((width, BLK), f32),
            pltpu.VMEM((slots, part), f32),
            pltpu.VMEM((2, chips, rows_part, width), bf16),
            pltpu.VMEM((pieces, BLK, width + 2 * LANES), bf16),
            pltpu.VMEM((2, slots + 2 * EDGE, LANES), f32),
            pltpu.VMEM((2, slots + 2 * EDGE, LANES), f32),
            pltpu.VMEM((slots + 2 * EDGE, LANES), f32),
            pltpu.VMEM((2, taps, LANES), f32),
            pltpu.VMEM((2, BLK, LANES), f32),
            pltpu.VMEM((2, slots, LANES), f32),
            pltpu.VMEM((2, slots, LANES), f32),
            pltpu.VMEM((part, slots), f32),
            pltpu.VMEM((part, slots), f32),
            pltpu.VMEM((2, taps, BLK, LANES), f32),
            pltpu.VMEM(own.shape, bf16),
            pltpu.VMEM(other.shape, bf16),
            pltpu.VMEM(input_weight.shape, bf16),
            pltpu.VMEM(delta.shape, bf16),
            pltpu.VMEM(output_weight.shape, bf16),
            pltpu.VMEM((width, slots), bf16),
            pltpu.VMEM((width, slots), bf16),
            pltpu.VMEM((slots, part), bf16),
            pltpu.VMEM((2, part, slots), bf16),
            pltpu.VMEM((chips, part + SIDE, slots), bf16),
            pltpu.VMEM((chips, part + SIDE, slots), bf16),
            pltpu.SemaphoreType.DMA((5,)),
            pltpu.SemaphoreType.DMA((8 + 2 * chips,)),
        ],
        1,
        3000000000,
        12000000,
        (1, 2, 5, 10, 11),
        (0, 1, 2, 3, 4, 5),
        60,
    )(
        scalars,
        own,
        other,
        norm_gain[None],
        norm_bias[None],
        input_weight,
        depth_weight,
        batch_scale[None],
        batch_shift[None],
        segment[None],
        delta,
        output_weight,
    )
    got = lax.ppermute(send_half, "core", SWAP)
    paired = full_call(
        pair_kernel, (sds(keep.shape[1:], bf16),) * chips, [], 1, 1000000, 2400000
    )(scalars, keep, got)
    terms = {0: paired[0]}
    for j in range(chips - 1, 0, -1):
        terms[j] = lax.ppermute(paired[j], "zl", [(z, z ^ j) for z in range(chips)])
    terms = [terms[j] for j in range(chips)]

    lines, peers = lax.axis_size("x"), lax.axis_size(("zh", "y"))
    grads = grads.reshape((lines, peers) + grads.shape[1:])
    grads = lax.all_to_all(grads, "x", split_axis=0, concat_axis=0, tiled=True)
    grads, *terms = lax.optimization_barrier((grads, *terms))
    grads = full_call(sum_kernel, sds(grads.shape[1:], bf16), [], 0, 1000000, 2300000)(grads)
    grads = lax.all_to_all(grads, ("zh", "y"), split_axis=0, concat_axis=0, tiled=True)

    mixed_send, *terms = lax.optimization_barrier((mixed_send, *terms))
    mixed = mixed_keep.astype(f32) + lax.ppermute(mixed_send, "core", SWAP).astype(f32)
    mixed = mixed.astype(bf16).reshape(chips * rows_part, width)
    mixed_sum = lax.psum_scatter(mixed, "zl", scatter_dimension=0, tiled=True)

    column_start = tensor_index * part
    gain_part = lax.dynamic_slice_in_dim(norm_gain, column_start, part)[None]
    delta_part = lax.dynamic_slice_in_dim(delta, column_start, part, 1)
    homebound = full_call(
        row_kernel,
        sds((count, BLK, 2 * LANES), bf16),
        [pltpu.VMEM((2, slots, LANES), f32)],
        1,
        1000000,
        1000000,
    )(scalars, *terms, packed, stats, gain_part, delta_part)
    wide = grads.shape[-1]
    shared = full_call(
        share_kernel, sds((peers, BLK, wide + lines * 2 * LANES), bf16), [], 0, 1000000, 1500000
    )(grads, homebound.reshape(peers, lines, BLK, 2 * LANES))
    shared = lax.all_to_all(shared, ("zh", "y"), split_axis=0, concat_axis=0, tiled=True)
    fanned = full_call(
        fan_kernel, sds((lines, peers, BLK, wide + 2 * LANES), bf16), [], 0, 1000000, 3000000
    )(shared)
    whole = lax.all_to_all(fanned, "x", split_axis=0, concat_axis=0, tiled=True)
    whole = whole.reshape((pieces,) + whole.shape[2:])
    target = lax.rem(target, lines) * peers + target // lines
    weight_grad, out_grad, tap_grad, side, frame_gradient = full_call(
        unpack_kernel,
        (
            sds((2 * part, width), bf16),
            sds((part, width), bf16),
            sds((taps, part), f32),
            sds((2, part), f32),
            sds((part, load_rows), bf16),
        ),
        [pltpu.VMEM((pieces, BLK, 2 * LANES), f32), pltpu.VMEM((load_rows, 2 * LANES), f32)],
        1,
        1000000,
        5000000,
    )(target, whole)
    weight_grad = weight_grad.reshape(2, part, width)
    frame_gradient = frame_gradient.T

    row_start = tensor_index * rows_part
    live_mine = (row_start + jnp.arange(rows_part, dtype=jnp.int32) < my_blocks * BLK)[:, None]
    residual = lax.dynamic_slice_in_dim(gathered, row_start, rows_part, 1).T
    block_output = jnp.where(
        live_mine, residual.astype(f32) + mixed_sum.astype(f32), 0.0
    ).astype(bf16)
    return (block_output, frame_gradient, weight_grad, out_grad, tap_grad, side[0], side[1])


def solution(mesh):
    fine = Mesh(mesh.devices.reshape(2, 8, 4, 4, 2), DP + TENSOR)
    in_specs = (
        P(DP, TENSOR),
        P(),
        P(),
        P(None, TENSOR, None),
        P(None, TENSOR),
        P(TENSOR),
        P(TENSOR),
        P(TENSOR, None),
        P(DP + TENSOR, None),
        P(),
        P(DP),
    )
    out_specs = (
        P(DP + TENSOR, None),
        P(DP, TENSOR),
        P(None, TENSOR, None),
        P(TENSOR, None),
        P(None, TENSOR),
        P(TENSOR),
        P(TENSOR),
    )
    return jax.shard_map(
        on_device, mesh=fine, in_specs=in_specs, out_specs=out_specs, check_vma=False
    )
```

```python
import functools

import jax
import jax.numpy as jnp
from jax import lax
from jax.experimental import pallas as pl
from jax.experimental.pallas import tpu as pltpu
from jax.sharding import Mesh
from jax.sharding import PartitionSpec as P

BLK = 8
LANES = 128
EDGE = 16
SIDE = 16
epsilon = 1e-05
MIB = 1024 * 1024

f32 = jnp.float32
bf16 = jnp.bfloat16
SWAP = ((0, 1), (1, 0))
DP = ("zh", "y", "x")
TENSOR = ("zl", "core")


def dot_general(a, b, ca, cb):
    return lax.dot_general(a, b, (((ca,), (cb,)), ((), ())), preferred_element_type=f32)


def full_call(kernel, out_shape, scratch, smem, flops, nbytes, copied=(), sent=(), room=16):
    def call(*args):
        specs = [pl.BlockSpec(memory_space=pltpu.SMEM)] * smem
        specs += [pl.BlockSpec(memory_space=pltpu.VMEM)] * (len(args) - smem)
        for place in copied:
            specs[place] = pl.BlockSpec(memory_space=pl.ANY)
        outs = jax.tree.map(lambda _: pl.BlockSpec(memory_space=pltpu.VMEM), out_shape)
        if sent:
            outs = tuple(
                pl.BlockSpec(memory_space=pl.ANY if k in sent else pltpu.VMEM)
                for k in range(len(out_shape))
            )
        return pl.pallas_call(
            kernel,
            out_shape=out_shape,
            in_specs=specs,
            out_specs=outs,
            scratch_shapes=scratch,
            compiler_params=pltpu.CompilerParams(vmem_limit_bytes=room * MIB),
            cost_estimate=pl.CostEstimate(flops=flops, bytes_accessed=nbytes, transcendentals=0),
        )(*args)

    return call


def outbox_kernel(replica_blocks, place, frames_hbm, out_ref, held, frames_t, sem):
    copy = pltpu.make_async_copy(frames_hbm, frames_t, sem)
    copy.start()
    part, rows = frames_t.shape
    count = out_ref.shape[0]
    copy.wait()
    for c in range(0, part, LANES):
        e = min(part, c + LANES)
        held[:, c:e] = jnp.transpose(frames_t[c:e, :].astype(f32))
    start = jnp.int32(0)
    for r in range(count):
        block = jnp.minimum(lax.div(start - place[0] + (count - 1), count), rows // BLK - 1)
        at = pl.ds(pl.multiple_of(block * BLK, BLK), BLK)
        out_ref[r] = held[at, :].astype(bf16)
        start = start + replica_blocks[r]


def pack_kernel(scalars, arrived, rows_out, cols_out, held):
    start, blocks = scalars[0], scalars[1]
    count, _, width = arrived.shape
    for p in range(count):
        block = arrived[lax.rem(start + p, count)].astype(f32)
        held[p * BLK : (p + 1) * BLK, :] = jnp.where(p < blocks, block, 0.0)
    rows = held[...]
    rows_out[...] = rows.astype(bf16)
    for c in range(0, width, LANES):
        e = min(width, c + LANES)
        cols_out[c:e, :] = jnp.transpose(held[:, c:e]).astype(bf16)


def split_rows(unit, cross):
    row = lax.broadcasted_iota(jnp.int32, (SIDE, unit.shape[1]), 0)
    out = jnp.zeros((SIDE, unit.shape[1]), f32)
    for k, value in enumerate((unit, cross)):
        high = value.astype(bf16).astype(f32)
        out = jnp.where(row == 2 * k, high, out)
        out = jnp.where(row == 2 * k + 1, value - high, out)
    return out.astype(bf16)


def main_kernel(
    scalars,
    own_hbm,
    other_hbm,
    gain_ref,
    bias_ref,
    win_hbm,
    taps_ref,
    scale_ref,
    shift_ref,
    seg_ref,
    delta_hbm,
    wout_hbm,
    x_hbm,
    keep_hbm,
    send_hbm,
    mixed_keep_hbm,
    mixed_send_hbm,
    grad_hbm,
    stats_ref,
    gb_ref,
    mixed_s,
    grad_ref,
    glu_s,
    dc_s,
    seg_s,
    w_s,
    bn_s,
    pre_s,
    dglu_s,
    lin_s,
    sig_s,
    tap_s,
    own_ref,
    other_ref,
    win_ref,
    delta_ref,
    wout_ref,
    x_ref,
    normed_ref,
    swish_ref,
    dlt_ref,
    keep_ref,
    send_ref,
    sems,
    out_sems,
):
    def send(k, source, target):
        copy = pltpu.make_async_copy(source, target, out_sems.at[k])
        copy.start()
        sends.append(copy)

    sends = []
    copies = [
        pltpu.make_async_copy(source, target, sems.at[k])
        for k, (source, target) in enumerate(
            (
                (own_hbm, own_ref),
                (other_hbm, other_ref),
                (win_hbm, win_ref),
                (delta_hbm, delta_ref),
                (wout_hbm, wout_ref),
            )
        )
    ]
    for copy in copies:
        copy.start()
    width, slots = x_ref.shape
    part = win_ref.shape[1]
    taps = taps_ref.shape[0]
    rest = part - LANES
    live = scalars[1] * BLK
    core = scalars[3]
    chunk = 64
    steps = width // chunk
    chips = own_ref.shape[0]
    per_part = part // chunk

    w_s[...] = jnp.zeros_like(w_s)
    w_s[0] = taps_ref[:, 0:LANES]
    w_s[1, :, 0:rest] = taps_ref[:, LANES:part]
    bn_s[...] = jnp.zeros_like(bn_s)
    bn_s[0, 0:1, :] = scale_ref[:, 0:LANES]
    bn_s[1, 0:1, 0:rest] = scale_ref[:, LANES:part]
    bn_s[0, 1:2, :] = shift_ref[:, 0:LANES]
    bn_s[1, 1:2, 0:rest] = shift_ref[:, LANES:part]
    row = lax.broadcasted_iota(jnp.int32, (BLK, width), 0)
    gb_ref[...] = jnp.transpose(jnp.where(row == 0, gain_ref[...], bias_ref[...]))
    segments = jnp.broadcast_to(seg_ref[...].astype(f32), (BLK, slots))
    seg_s[...] = jnp.full(seg_s.shape, -1.0, f32)
    seg_s[EDGE : EDGE + slots, :] = jnp.broadcast_to(jnp.transpose(segments)[:, 0:1], (slots, LANES))

    glu_s[...] = jnp.zeros_like(glu_s)
    dc_s[...] = jnp.zeros_like(dc_s)
    tap_s[...] = jnp.zeros_like(tap_s)

    copies[0].wait()
    copies[1].wait()

    def fold(v):
        return jnp.sum(v.reshape(chunk // BLK, BLK, slots), axis=0)

    def sum_body(i, acc):
        chip, row = i // per_part, pl.multiple_of(lax.rem(i, per_part) * chunk, chunk)
        for ref, c in ((own_ref, core), (other_ref, 1 - core)):
            value = ref[chip, pl.ds(row, chunk), :]
            to = pl.multiple_of((2 * chip + c) * part + row, chunk)
            x_ref[pl.ds(to, chunk), :] = value
            acc = acc + fold(value.astype(f32))
        return acc

    zero = jnp.zeros((BLK, slots), f32)
    center = lax.fori_loop(0, chips * per_part, sum_body, zero)
    center = jnp.sum(center, axis=0, keepdims=True) / width

    send(0, x_ref, x_hbm)

    def square_body(i, acc):
        return acc + fold(jnp.square(x_ref[pl.ds(i * chunk, chunk), :].astype(f32) - center))

    spread = jnp.sum(lax.fori_loop(0, steps, square_body, zero, unroll=2), axis=0, keepdims=True) / width
    row_scale = lax.rsqrt(spread + epsilon)
    stats_ref[...] = jnp.zeros_like(stats_ref)
    stats_ref[0:1, :] = center
    stats_ref[1:2, :] = row_scale

    def norm_body(i, carry):
        at = pl.ds(i * chunk, chunk)
        standard = (x_ref[at, :].astype(f32) - center) * row_scale
        normed_ref[at, :] = (standard * gb_ref[at, 0:1] + gb_ref[at, 1:2]).astype(bf16)
        return carry

    lax.fori_loop(0, steps, norm_body, 0, unroll=2)


    copies[2].wait()
    normed = normed_ref[...]
    linear = dot_general(win_ref[0], normed, 1, 0)
    gate_sigmoid = jax.nn.sigmoid(dot_general(win_ref[1], normed, 1, 0))
    lin_s[...] = linear
    sig_s[...] = gate_sigmoid
    is_live = lax.broadcasted_iota(jnp.int32, (part, slots), 1) < live
    glu = jnp.where(is_live, (linear * gate_sigmoid).astype(bf16).astype(f32), 0.0)
    glu_s[0, EDGE : EDGE + slots, :] = jnp.transpose(glu[0:LANES])
    glu_s[1, EDGE : EDGE + slots, 0:rest] = jnp.transpose(glu[LANES:part])

    rows = 64
    blocks = slots // rows
    copies[3].wait()
    copies[4].wait()

    def conv_body(i, carry):
        base = pl.multiple_of(i * rows, rows)
        here = seg_s[pl.ds(base + EDGE, rows), :]
        acc = [jnp.zeros((rows, LANES), f32) for _ in range(2)]
        for j in range(taps):
            same = seg_s[pl.ds(base + j, rows), :] == here
            for h in range(2):
                value = jnp.where(same, glu_s[h, pl.ds(base + j, rows), :], 0.0)
                acc[h] = acc[h] + value * w_s[h, j : j + 1, :]
        for h in range(2):
            pre_s[h, pl.ds(base, rows), :] = acc[h] * bn_s[h, 0:1, :] + bn_s[h, 1:2, :]
        return carry

    lax.fori_loop(0, blocks, conv_body, 0)

    delta_swish = dot_general(delta_ref[...], wout_ref[...], 1, 1)
    row_live = lax.broadcasted_iota(jnp.int32, (slots, LANES), 0) < live
    for h in range(2):
        pre = pre_s[h]
        s = jax.nn.sigmoid(pre)
        swish = jnp.where(row_live, pre * s, 0.0).astype(bf16)
        slope = jnp.where(row_live, s * (1.0 + pre * (1.0 - s)) * bn_s[h, 0:1, :], 0.0)
        if h == 0:
            swish_ref[:, 0:LANES] = swish
            dc_s[h, EDGE : EDGE + slots, :] = delta_swish[:, 0:LANES] * slope
        else:
            swish_ref[:, LANES:part] = swish[:, 0:rest]
            dc_s[h, EDGE : EDGE + slots, 0:rest] = delta_swish[:, LANES:part] * slope[:, 0:rest]

    swish_t = jnp.transpose(swish_ref[...].astype(f32)).astype(bf16)


    def back_body(i, carry):
        base = pl.multiple_of(i * rows, rows)
        mixed = dot_general(swish_ref[pl.ds(base, rows), :], wout_ref[...], 1, 0)
        mixed_s[lax.rem(i, 2) ^ core, i // 2] = mixed.astype(bf16)
        here = seg_s[pl.ds(base + EDGE, rows), :]
        alive = (base + lax.broadcasted_iota(jnp.int32, (rows, LANES), 0)) < live
        glu_here = [glu_s[h, pl.ds(base + EDGE, rows), :] for h in range(2)]
        acc = [jnp.zeros((rows, LANES), f32) for _ in range(2)]
        for j in range(taps):
            at = pl.ds(base + (2 * EDGE - j), rows)
            same = seg_s[at, :] == here
            for h in range(2):
                value = jnp.where(same, dc_s[h, at, :], 0.0)
                acc[h] = acc[h] + value * w_s[h, j : j + 1, :]
                tap_s[h, j] += jnp.sum((value * glu_here[h]).reshape(rows // BLK, BLK, LANES), axis=0)
        for h in range(2):
            dglu_s[h, pl.ds(base, rows), :] = jnp.where(alive, acc[h], 0.0)
        return carry

    lax.fori_loop(0, blocks, back_body, 0)
    send(1, mixed_s.at[0], mixed_keep_hbm)
    send(2, mixed_s.at[1], mixed_send_hbm)

    per = part // BLK
    parts = grad_ref.shape[0]
    extra = grad_ref.shape[2] - width
    left = parts - 2 * per
    cols = 512
    for d in range(0, width, cols):
        block = dot_general(swish_t, delta_ref[:, d : d + cols], 1, 0).astype(bf16)
        grad_ref[2 * per : parts, :, d : d + cols] = block[0 : left * BLK].reshape(left, BLK, cols)
        over = block[left * BLK :].reshape(per - left, BLK, cols)
        for r in range(per - left):
            for c in range(0, cols, extra):
                at = r * (width // extra) + (d + c) // extra
                grad_ref[at, :, width : width + extra] = over[r, :, c : c + extra]
    first = (per - left) * (width // extra)
    grad_ref[first:parts, :, width : width + extra] = jnp.zeros((parts - first, BLK, extra), bf16)
    for h, (c, e) in enumerate(((0, LANES), (LANES, part))):
        tap = jnp.sum(tap_s[h], axis=1)[:, 0 : e - c].astype(bf16)
        for r in range(taps // BLK):
            grad_ref[first + r, :, width + c : width + e] = tap[r * BLK : (r + 1) * BLK]

    def depart(k, begin, end):
        send(k, grad_ref.at[begin:end], grad_hbm.at[begin:end])

    depart(3, 2 * per, parts)

    for h, (c, e) in enumerate(((0, LANES), (LANES, part))):
        dglu = jnp.transpose(dglu_s[h])[0 : e - c]
        s = sig_s[c:e, :]
        dlt_ref[0, c:e, :] = (dglu * s).astype(bf16)
        dlt_ref[1, c:e, :] = (dglu * lin_s[c:e, :] * s * (1.0 - s)).astype(bf16)


    for k in range(2):
        for d in range(0, width, cols):
            block = dot_general(dlt_ref[k], normed_ref[d : d + cols, :], 1, 1).astype(bf16)
            grad_ref[k * per : (k + 1) * per, :, d : d + cols] = block.reshape(per, BLK, cols)
        depart(4 + k, k * per, (k + 1) * per)

    unit = jnp.zeros((BLK, slots), f32)
    cross = jnp.zeros((BLK, slots), f32)
    wide = 2 * part
    for z in range(chips):
        d = z * wide
        term = dot_general(win_ref[0, :, d : d + wide], dlt_ref[0], 0, 0)
        term = term + dot_general(win_ref[1, :, d : d + wide], dlt_ref[1], 0, 0)
        term = term.astype(bf16)
        first, second = term[0:part], term[part:wide]
        send_ref[z, 0:part, :] = jnp.where(core == 0, second, first)
        send(6 + z, send_ref.at[z, 0:part], send_hbm.at[z, 0:part])
        keep_ref[z, 0:part, :] = jnp.where(core == 0, first, second)
        send(6 + chips + z, keep_ref.at[z, 0:part], keep_hbm.at[z, 0:part])
        weighted = term.astype(f32) * gb_ref[d : d + wide, 0:1]
        standard = (x_ref[d : d + wide, :].astype(f32) - center) * row_scale
        unit = unit + jnp.sum(weighted.reshape(wide // BLK, BLK, slots), axis=0)
        cross = cross + jnp.sum((weighted * standard).reshape(wide // BLK, BLK, slots), axis=0)
    totals = split_rows(
        jnp.sum(unit, axis=0, keepdims=True), jnp.sum(cross, axis=0, keepdims=True)
    )
    for z in range(chips):
        send_ref[z, part : part + SIDE, :] = totals
        keep_ref[z, part : part + SIDE, :] = totals
    below = pl.ds(part, SIDE)
    send(6 + 2 * chips, send_ref.at[:, below], send_hbm.at[:, below])
    send(7 + 2 * chips, keep_ref.at[:, below], keep_hbm.at[:, below])
    for copy in sends:
        copy.wait()


def pair_kernel(scalars, keep_ref, got_ref, *outs):
    chips, rows, _ = keep_ref.shape
    part = rows - SIDE
    side = keep_ref[0, part:rows, :].astype(f32) + got_ref[0, part:rows, :].astype(f32)
    totals = split_rows(side[0:1] + side[1:2], side[2:3] + side[3:4])
    for j in range(chips):
        z = scalars[4] ^ j
        total = keep_ref[z, 0:part, :].astype(f32) + got_ref[z, 0:part, :].astype(f32)
        outs[j][0:part, :] = total.astype(bf16)
        outs[j][part:rows, :] = totals


def sum_kernel(in_ref, out_ref):
    for k in range(out_ref.shape[0]):
        total = sum(in_ref[i, k].astype(f32) for i in range(in_ref.shape[0]))
        out_ref[k] = total.astype(bf16)


def share_kernel(in_ref, home_ref, out_ref):
    peers, _, wide = in_ref.shape
    lines = home_ref.shape[1]
    total = sum(in_ref[i].astype(f32) for i in range(peers)).astype(bf16)
    for i in range(peers):
        out_ref[i, :, 0:wide] = total
        for k in range(lines):
            at = wide + k * 2 * LANES
            out_ref[i, :, at : at + 2 * LANES] = home_ref[i, k]


def unpack_kernel(target, in_ref, weight_ref, out_ref, tap_ref, side_ref, frame_ref, held, turned_rows):
    pieces, _, full = in_ref.shape
    taps, part = tap_ref.shape
    width = weight_ref.shape[1]
    wide = full - 2 * LANES
    extra = wide - width
    per = part // BLK
    left = pieces - 2 * per
    cols = 2 * extra
    for d in range(0, width, cols):
        weight_ref[:, d : d + cols] = in_ref[0 : 2 * per, :, d : d + cols].reshape(2 * part, cols)
        out_ref[0 : left * BLK, d : d + cols] = in_ref[2 * per : pieces, :, d : d + cols].reshape(
            left * BLK, cols
        )
    for c in range(0, width, extra):
        rows = [in_ref[r * (width // extra) + c // extra, :, width:wide] for r in range(per - left)]
        out_ref[left * BLK : part, c : c + extra] = jnp.concatenate(rows, axis=0)
    first = (per - left) * (width // extra)
    for r in range(taps // BLK):
        tap_ref[r * BLK : (r + 1) * BLK, :] = in_ref[first + r, :, width : width + part].astype(f32)
    total = jnp.zeros((BLK, LANES), f32)
    for s in range(pieces):
        held[s] = in_ref[s, :, wide:full].astype(f32)
        total = total + held[s, :, LANES:]
    turned = pltpu.roll(total, LANES - part % LANES, 1)
    low = lax.broadcasted_iota(jnp.int32, (1, LANES), 1) < part % LANES
    for k in range(2):
        side_ref[k : k + 1, 0:LANES] = jnp.where(
            low, turned[3 * k : 3 * k + 1], total[3 * k + 1 : 3 * k + 2]
        )
        side_ref[k : k + 1, LANES:part] = turned[3 * k + 2 : 3 * k + 3, 0 : part - LANES]
    for k in range(frame_ref.shape[1] // BLK):
        turned_rows[k * BLK : (k + 1) * BLK, :] = held[target[k]]
    for c in range(0, part, LANES):
        e = min(part, c + LANES)
        frame_ref[c:e, :] = jnp.transpose(turned_rows[:, c:e]).astype(bf16)


def fan_kernel(in_ref, out_ref):
    lines, peers, _, full = out_ref.shape
    wide = full - 2 * LANES
    for i in range(peers):
        piece = in_ref[i, :, 0:wide]
        for k in range(lines):
            at = wide + k * 2 * LANES
            out_ref[k, i, :, 0:wide] = piece
            out_ref[k, i, :, wide:full] = in_ref[i, :, at : at + 2 * LANES]


def row_kernel(scalars, dn0, dn1, dn2, dn3, x_ref, stats_ref, gain_ref, delta_ref, out_ref, held):
    start, blocks = scalars[0], scalars[1]
    terms = (dn0, dn1, dn2, dn3)
    slots, part = x_ref.shape
    width = scalars[2].astype(f32)
    rest = part - LANES
    count = slots // BLK
    live = blocks * BLK
    totals = sum(term[part : part + SIDE, :].astype(f32) for term in terms)
    unit, cross = totals[0:1] + totals[1:2], totals[2:3] + totals[3:4]
    row = lax.broadcasted_iota(jnp.int32, (BLK, slots), 0)
    side = jnp.where(row == 2, unit, jnp.where(row == 3, cross, stats_ref[...]))
    side = jnp.transpose(side)
    center, row_scale = side[:, 0:1], side[:, 1:2]
    unit, cross = side[:, 2:3] / width, side[:, 3:4] / width
    sums = []
    for h, (c, e) in enumerate(((0, LANES), (LANES, part))):
        dn = jnp.transpose(sum(term[c:e, :].astype(f32) for term in terms))
        standard = (x_ref[:, c:e].astype(f32) - center) * row_scale
        sums.append((jnp.sum(dn * standard, axis=0, keepdims=True), jnp.sum(dn, axis=0, keepdims=True)))
        on = lax.broadcasted_iota(jnp.int32, (slots, e - c), 0) < live
        own = jnp.where(on, delta_ref[:, c:e].astype(f32), 0.0)
        held[h, :, 0 : e - c] = own + row_scale * (dn * gain_ref[:, c:e] - unit - standard * cross)
    held[1, :, rest:LANES] = jnp.zeros((slots, LANES - rest), f32)
    row = lax.broadcasted_iota(jnp.int32, (BLK, LANES), 0)
    lane = lax.broadcasted_iota(jnp.int32, (BLK, LANES), 1)
    beside = jnp.zeros((BLK, LANES), f32)
    for k in range(2):
        low = jnp.broadcast_to(sums[0][k], (BLK, LANES))
        high = jnp.broadcast_to(jnp.concatenate([sums[1][k], sums[1][k]], axis=1), (BLK, LANES))
        beside = jnp.where(row == 3 * k, pltpu.roll(low, 64, 1), beside)
        beside = jnp.where(row == 3 * k + 1, low, beside)
        beside = jnp.where(row == 3 * k + 2, high, beside)
    for s in range(count):
        at = pl.ds(pl.multiple_of(lax.rem(s - start + 16 * count, count) * BLK, BLK), BLK)
        out_ref[s, :, 0:LANES] = held[0, at, :].astype(bf16)
        out_ref[s, :, LANES : 2 * LANES] = jnp.where(lane < rest, held[1, at, :], beside).astype(bf16)


def on_device(
    frames,
    norm_gain,
    norm_bias,
    input_weight,
    depth_weight,
    batch_scale,
    batch_shift,
    output_weight,
    upstream,
    replica_blocks,
    segment,
):
    replicas = lax.axis_size(DP)
    my_index = lax.axis_index(DP)
    tensor_index = lax.axis_index(TENSOR)
    width = norm_gain.shape[0]
    load_rows, part = frames.shape
    slots = segment.shape[0]
    rows_part = upstream.shape[0]
    taps = depth_weight.shape[0]
    load_blocks = load_rows // BLK
    count = slots // BLK

    delta = lax.all_gather(upstream, TENSOR, axis=0, tiled=True)

    ends = jnp.cumsum(replica_blocks)
    starts = ends - replica_blocks
    numbers = my_index + replicas * jnp.arange(load_blocks, dtype=jnp.int32)
    target = jnp.sum((ends[None, :] <= numbers[:, None]).astype(jnp.int32), axis=1)
    is_mine = jnp.arange(replicas, dtype=jnp.int32) == my_index
    my_start = jnp.sum(jnp.where(is_mine, starts, 0))
    my_blocks = jnp.sum(jnp.where(is_mine, replica_blocks, 0))
    core = lax.axis_index("core")
    scalars = jnp.stack([lax.rem(my_start, replicas), my_blocks, jnp.int32(width), core, lax.axis_index("zl")])

    sds = jax.ShapeDtypeStruct
    outbox = full_call(
        outbox_kernel,
        sds((replicas, BLK, part), bf16),
        [
            pltpu.VMEM((load_rows, part), f32),
            pltpu.VMEM((part, load_rows), bf16),
            pltpu.SemaphoreType.DMA(()),
        ],
        2,
        1000,
        400000,
        (2,),
    )(replica_blocks, my_index[None], frames.T)
    arrived = lax.all_to_all(outbox, DP, split_axis=0, concat_axis=0, tiled=True)

    packed, packed_t = full_call(
        pack_kernel,
        (sds((slots, part), bf16), sds((part, slots), bf16)),
        [pltpu.VMEM((slots, part), f32)],
        1,
        1000,
        1000000,
    )(scalars, arrived)
    own = lax.all_gather(packed_t, "zl", axis=0)
    other = lax.ppermute(own, "core", SWAP)
    chips = own.shape[0]

    pieces = replicas
    half = sds((chips, rows_part, width), bf16)
    gathered, keep, send_half, mixed_keep, mixed_send, grads, stats = full_call(
        main_kernel,
        (
            sds((width, slots), bf16),
            sds((chips, part + SIDE, slots), bf16),
            sds((chips, part + SIDE, slots), bf16),
            half,
            half,
            sds((pieces, BLK, width + 2 * LANES), bf16),
            sds((BLK, slots), f32),
        ),
        [
            pltpu.VMEM((width, BLK), f32),
            pltpu.VMEM((2, chips, rows_part, width), bf16),
            pltpu.VMEM((pieces, BLK, width + 2 * LANES), bf16),
            pltpu.VMEM((2, slots + 2 * EDGE, LANES), f32),
            pltpu.VMEM((2, slots + 2 * EDGE, LANES), f32),
            pltpu.VMEM((slots + 2 * EDGE, LANES), f32),
            pltpu.VMEM((2, taps, LANES), f32),
            pltpu.VMEM((2, BLK, LANES), f32),
            pltpu.VMEM((2, slots, LANES), f32),
            pltpu.VMEM((2, slots, LANES), f32),
            pltpu.VMEM((part, slots), f32),
            pltpu.VMEM((part, slots), f32),
            pltpu.VMEM((2, taps, BLK, LANES), f32),
            pltpu.VMEM(own.shape, bf16),
            pltpu.VMEM(other.shape, bf16),
            pltpu.VMEM(input_weight.shape, bf16),
            pltpu.VMEM(delta.shape, bf16),
            pltpu.VMEM(output_weight.shape, bf16),
            pltpu.VMEM((width, slots), bf16),
            pltpu.VMEM((width, slots), bf16),
            pltpu.VMEM((slots, part), bf16),
            pltpu.VMEM((2, part, slots), bf16),
            pltpu.VMEM((chips, part + SIDE, slots), bf16),
            pltpu.VMEM((chips, part + SIDE, slots), bf16),
            pltpu.SemaphoreType.DMA((5,)),
            pltpu.SemaphoreType.DMA((8 + 2 * chips,)),
        ],
        1,
        3000000000,
        12000000,
        (1, 2, 5, 10, 11),
        (0, 1, 2, 3, 4, 5),
        60,
    )(
        scalars,
        own,
        other,
        norm_gain[None],
        norm_bias[None],
        input_weight,
        depth_weight,
        batch_scale[None],
        batch_shift[None],
        segment[None],
        delta,
        output_weight,
    )
    got = lax.ppermute(send_half, "core", SWAP)
    paired = full_call(
        pair_kernel, (sds(keep.shape[1:], bf16),) * chips, [], 1, 1000000, 2400000
    )(scalars, keep, got)
    terms = {0: paired[0]}
    for j in range(chips - 1, 0, -1):
        terms[j] = lax.ppermute(paired[j], "zl", [(z, z ^ j) for z in range(chips)])
    terms = [terms[j] for j in (0, 3, 2, 1)]

    lines, peers = lax.axis_size("x"), lax.axis_size(("zh", "y"))
    grads = grads.reshape((lines, peers) + grads.shape[1:])
    grads = lax.all_to_all(grads, "x", split_axis=0, concat_axis=0, tiled=True)
    grads, *terms = lax.optimization_barrier((grads, *terms))
    grads = full_call(sum_kernel, sds(grads.shape[1:], bf16), [], 0, 1000000, 2300000)(grads)
    grads = lax.all_to_all(grads, ("zh", "y"), split_axis=0, concat_axis=0, tiled=True)

    mixed_send, *terms = lax.optimization_barrier((mixed_send, *terms))
    mixed = mixed_keep.astype(f32) + lax.ppermute(mixed_send, "core", SWAP).astype(f32)
    mixed = mixed.astype(bf16).reshape(chips * rows_part, width)
    mixed_sum = lax.psum_scatter(mixed, "zl", scatter_dimension=0, tiled=True)

    column_start = tensor_index * part
    gain_part = lax.dynamic_slice_in_dim(norm_gain, column_start, part)[None]
    delta_part = lax.dynamic_slice_in_dim(delta, column_start, part, 1)
    homebound = full_call(
        row_kernel,
        sds((count, BLK, 2 * LANES), bf16),
        [pltpu.VMEM((2, slots, LANES), f32)],
        1,
        1000000,
        1000000,
    )(scalars, *terms, packed, stats, gain_part, delta_part)
    wide = grads.shape[-1]
    shared = full_call(
        share_kernel, sds((peers, BLK, wide + lines * 2 * LANES), bf16), [], 0, 1000000, 1500000
    )(grads, homebound.reshape(peers, lines, BLK, 2 * LANES))
    shared = lax.all_to_all(shared, ("zh", "y"), split_axis=0, concat_axis=0, tiled=True)
    fanned = full_call(
        fan_kernel, sds((lines, peers, BLK, wide + 2 * LANES), bf16), [], 0, 1000000, 3000000
    )(shared)
    whole = lax.all_to_all(fanned, "x", split_axis=0, concat_axis=0, tiled=True)
    whole = whole.reshape((pieces,) + whole.shape[2:])
    target = lax.rem(target, lines) * peers + target // lines
    weight_grad, out_grad, tap_grad, side, frame_gradient = full_call(
        unpack_kernel,
        (
            sds((2 * part, width), bf16),
            sds((part, width), bf16),
            sds((taps, part), f32),
            sds((2, part), f32),
            sds((part, load_rows), bf16),
        ),
        [pltpu.VMEM((pieces, BLK, 2 * LANES), f32), pltpu.VMEM((load_rows, 2 * LANES), f32)],
        1,
        1000000,
        5000000,
    )(target, whole)
    weight_grad = weight_grad.reshape(2, part, width)
    frame_gradient = frame_gradient.T

    row_start = tensor_index * rows_part
    live_mine = (row_start + jnp.arange(rows_part, dtype=jnp.int32) < my_blocks * BLK)[:, None]
    residual = lax.dynamic_slice_in_dim(gathered, row_start, rows_part, 1).T
    block_output = jnp.where(
        live_mine, residual.astype(f32) + mixed_sum.astype(f32), 0.0
    ).astype(bf16)
    return (block_output, frame_gradient, weight_grad, out_grad, tap_grad, side[0], side[1])


def solution(mesh):
    fine = Mesh(mesh.devices.reshape(2, 8, 4, 4, 2), DP + TENSOR)
    in_specs = (
        P(DP, TENSOR),
        P(),
        P(),
        P(None, TENSOR, None),
        P(None, TENSOR),
        P(TENSOR),
        P(TENSOR),
        P(TENSOR, None),
        P(DP + TENSOR, None),
        P(),
        P(DP),
    )
    out_specs = (
        P(DP + TENSOR, None),
        P(DP, TENSOR),
        P(None, TENSOR, None),
        P(TENSOR, None),
        P(None, TENSOR),
        P(TENSOR),
        P(TENSOR),
    )
    return jax.shard_map(
        on_device, mesh=fine, in_specs=in_specs, out_specs=out_specs, check_vma=False
    )
```

```python
import functools

import jax
import jax.numpy as jnp
from jax import lax
from jax.experimental import pallas as pl
from jax.experimental.pallas import tpu as pltpu
from jax.sharding import Mesh
from jax.sharding import PartitionSpec as P

BLK = 8
LANES = 128
EDGE = 16
SIDE = 16
epsilon = 1e-05
MIB = 1024 * 1024

f32 = jnp.float32
bf16 = jnp.bfloat16
SWAP = ((0, 1), (1, 0))
DP = ("zh", "y", "x")
TENSOR = ("zl", "core")


def dot_general(a, b, ca, cb):
    return lax.dot_general(a, b, (((ca,), (cb,)), ((), ())), preferred_element_type=f32)


def full_call(kernel, out_shape, scratch, smem, flops, nbytes, copied=(), sent=(), room=16):
    def call(*args):
        specs = [pl.BlockSpec(memory_space=pltpu.SMEM)] * smem
        specs += [pl.BlockSpec(memory_space=pltpu.VMEM)] * (len(args) - smem)
        for place in copied:
            specs[place] = pl.BlockSpec(memory_space=pltpu.HBM)
        outs = jax.tree.map(lambda _: pl.BlockSpec(memory_space=pltpu.VMEM), out_shape)
        if sent:
            outs = tuple(
                pl.BlockSpec(memory_space=pltpu.HBM if k in sent else pltpu.VMEM)
                for k in range(len(out_shape))
            )
        return pl.pallas_call(
            kernel,
            out_shape=out_shape,
            in_specs=specs,
            out_specs=outs,
            scratch_shapes=scratch,
            compiler_params=pltpu.CompilerParams(vmem_limit_bytes=room * MIB),
            cost_estimate=pl.CostEstimate(flops=flops, bytes_accessed=nbytes, transcendentals=0),
        )(*args)

    return call


def outbox_kernel(replica_blocks, place, frames_hbm, out_ref, held, frames_t, sem):
    copy = pltpu.make_async_copy(frames_hbm, frames_t, sem)
    copy.start()
    part, rows = frames_t.shape
    count = out_ref.shape[0]
    copy.wait()
    for c in range(0, part, LANES):
        e = min(part, c + LANES)
        held[:, c:e] = jnp.transpose(frames_t[c:e, :].astype(f32))
    start = jnp.int32(0)
    for r in range(count):
        block = jnp.minimum(lax.div(start - place[0] + (count - 1), count), rows // BLK - 1)
        at = pl.ds(pl.multiple_of(block * BLK, BLK), BLK)
        out_ref[r] = held[at, :].astype(bf16)
        start = start + replica_blocks[r]


def pack_kernel(scalars, arrived, rows_out, cols_out, held):
    start, blocks = scalars[0], scalars[1]
    count, _, width = arrived.shape
    for p in range(count):
        block = arrived[lax.rem(start + p, count)].astype(f32)
        held[p * BLK : (p + 1) * BLK, :] = jnp.where(p < blocks, block, 0.0)
    rows = held[...]
    rows_out[...] = rows.astype(bf16)
    for c in range(0, width, LANES):
        e = min(width, c + LANES)
        cols_out[c:e, :] = jnp.transpose(held[:, c:e]).astype(bf16)


def split_rows(unit, cross):
    row = lax.broadcasted_iota(jnp.int32, (SIDE, unit.shape[1]), 0)
    out = jnp.zeros((SIDE, unit.shape[1]), f32)
    for k, value in enumerate((unit, cross)):
        high = value.astype(bf16).astype(f32)
        out = jnp.where(row == 2 * k, high, out)
        out = jnp.where(row == 2 * k + 1, value - high, out)
    return out.astype(bf16)


def main_kernel(
    scalars,
    own_hbm,
    other_hbm,
    gain_ref,
    bias_ref,
    win_hbm,
    taps_ref,
    scale_ref,
    shift_ref,
    seg_ref,
    delta_hbm,
    wout_hbm,
    x_hbm,
    keep_hbm,
    send_hbm,
    mixed_keep_hbm,
    mixed_send_hbm,
    grad_hbm,
    stats_ref,
    gb_ref,
    mixed_s,
    grad_ref,
    glu_s,
    dc_s,
    seg_s,
    w_s,
    bn_s,
    pre_s,
    dglu_s,
    lin_s,
    sig_s,
    tap_s,
    own_ref,
    other_ref,
    win_ref,
    delta_ref,
    wout_ref,
    x_ref,
    normed_ref,
    swish_ref,
    dlt_ref,
    keep_ref,
    send_ref,
    sems,
    out_sems,
):
    def send(k, source, target):
        copy = pltpu.make_async_copy(source, target, out_sems.at[k])
        copy.start()
        sends.append(copy)

    sends = []
    copies = [
        pltpu.make_async_copy(source, target, sems.at[k])
        for k, (source, target) in enumerate(
            (
                (own_hbm, own_ref),
                (other_hbm, other_ref),
                (win_hbm, win_ref),
                (delta_hbm, delta_ref),
                (wout_hbm, wout_ref),
            )
        )
    ]
    for copy in copies:
        copy.start()
    width, slots = x_ref.shape
    part = win_ref.shape[1]
    taps = taps_ref.shape[0]
    rest = part - LANES
    live = scalars[1] * BLK
    core = scalars[3]
    chunk = 64
    steps = width // chunk
    chips = own_ref.shape[0]
    per_part = part // chunk

    w_s[...] = jnp.zeros_like(w_s)
    w_s[0] = taps_ref[:, 0:LANES]
    w_s[1, :, 0:rest] = taps_ref[:, LANES:part]
    bn_s[...] = jnp.zeros_like(bn_s)
    bn_s[0, 0:1, :] = scale_ref[:, 0:LANES]
    bn_s[1, 0:1, 0:rest] = scale_ref[:, LANES:part]
    bn_s[0, 1:2, :] = shift_ref[:, 0:LANES]
    bn_s[1, 1:2, 0:rest] = shift_ref[:, LANES:part]
    row = lax.broadcasted_iota(jnp.int32, (BLK, width), 0)
    gb_ref[...] = jnp.transpose(jnp.where(row == 0, gain_ref[...], bias_ref[...]))
    segments = jnp.broadcast_to(seg_ref[...].astype(f32), (BLK, slots))
    seg_s[...] = jnp.full(seg_s.shape, -1.0, f32)
    seg_s[EDGE : EDGE + slots, :] = jnp.broadcast_to(jnp.transpose(segments)[:, 0:1], (slots, LANES))

    glu_s[...] = jnp.zeros_like(glu_s)
    dc_s[...] = jnp.zeros_like(dc_s)
    tap_s[...] = jnp.zeros_like(tap_s)

    copies[0].wait()
    copies[1].wait()

    def fold(v):
        return jnp.sum(v.reshape(chunk // BLK, BLK, slots), axis=0)

    def sum_body(i, acc):
        chip, row = i // per_part, pl.multiple_of(lax.rem(i, per_part) * chunk, chunk)
        for ref, c in ((own_ref, core), (other_ref, 1 - core)):
            value = ref[chip, pl.ds(row, chunk), :]
            to = pl.multiple_of((2 * chip + c) * part + row, chunk)
            x_ref[pl.ds(to, chunk), :] = value
            acc = acc + fold(value.astype(f32))
        return acc

    zero = jnp.zeros((BLK, slots), f32)
    center = lax.fori_loop(0, chips * per_part, sum_body, zero)
    center = jnp.sum(center, axis=0, keepdims=True) / width

    send(0, x_ref, x_hbm)

    def square_body(i, acc):
        return acc + fold(jnp.square(x_ref[pl.ds(i * chunk, chunk), :].astype(f32) - center))

    spread = jnp.sum(lax.fori_loop(0, steps, square_body, zero, unroll=8), axis=0, keepdims=True) / width
    row_scale = lax.rsqrt(spread + epsilon)
    stats_ref[...] = jnp.zeros_like(stats_ref)
    stats_ref[0:1, :] = center
    stats_ref[1:2, :] = row_scale

    def norm_body(i, carry):
        at = pl.ds(i * chunk, chunk)
        standard = (x_ref[at, :].astype(f32) - center) * row_scale
        normed_ref[at, :] = (standard * gb_ref[at, 0:1] + gb_ref[at, 1:2]).astype(bf16)
        return carry

    lax.fori_loop(0, steps, norm_body, 0, unroll=8)


    copies[2].wait()
    normed = normed_ref[...]
    linear = dot_general(win_ref[0], normed, 1, 0)
    gate_sigmoid = jax.nn.sigmoid(dot_general(win_ref[1], normed, 1, 0))
    lin_s[...] = linear
    sig_s[...] = gate_sigmoid
    is_live = lax.broadcasted_iota(jnp.int32, (part, slots), 1) < live
    glu = jnp.where(is_live, (linear * gate_sigmoid).astype(bf16).astype(f32), 0.0)
    glu_s[0, EDGE : EDGE + slots, :] = jnp.transpose(glu[0:LANES])
    glu_s[1, EDGE : EDGE + slots, 0:rest] = jnp.transpose(glu[LANES:part])

    rows = 64
    blocks = slots // rows
    copies[3].wait()
    copies[4].wait()

    def conv_body(i, carry):
        base = pl.multiple_of(i * rows, rows)
        here = seg_s[pl.ds(base + EDGE, rows), :]
        acc = [jnp.zeros((rows, LANES), f32) for _ in range(2)]
        for j in range(taps):
            same = seg_s[pl.ds(base + j, rows), :] == here
            for h in range(2):
                value = jnp.where(same, glu_s[h, pl.ds(base + j, rows), :], 0.0)
                acc[h] = acc[h] + value * w_s[h, j : j + 1, :]
        for h in range(2):
            pre_s[h, pl.ds(base, rows), :] = acc[h] * bn_s[h, 0:1, :] + bn_s[h, 1:2, :]
        return carry

    lax.fori_loop(0, blocks, conv_body, 0)

    delta_swish = dot_general(delta_ref[...], wout_ref[...], 1, 1)
    row_live = lax.broadcasted_iota(jnp.int32, (slots, LANES), 0) < live
    for h in range(2):
        pre = pre_s[h]
        s = jax.nn.sigmoid(pre)
        swish = jnp.where(row_live, pre * s, 0.0).astype(bf16)
        slope = jnp.where(row_live, s * (1.0 + pre * (1.0 - s)) * bn_s[h, 0:1, :], 0.0)
        if h == 0:
            swish_ref[:, 0:LANES] = swish
            dc_s[h, EDGE : EDGE + slots, :] = delta_swish[:, 0:LANES] * slope
        else:
            swish_ref[:, LANES:part] = swish[:, 0:rest]
            dc_s[h, EDGE : EDGE + slots, 0:rest] = delta_swish[:, LANES:part] * slope[:, 0:rest]

    swish_t = jnp.transpose(swish_ref[...].astype(f32)).astype(bf16)


    def back_body(i, carry):
        base = pl.multiple_of(i * rows, rows)
        mixed = dot_general(swish_ref[pl.ds(base, rows), :], wout_ref[...], 1, 0)
        mixed_s[lax.rem(i, 2) ^ core, i // 2] = mixed.astype(bf16)
        here = seg_s[pl.ds(base + EDGE, rows), :]
        alive = (base + lax.broadcasted_iota(jnp.int32, (rows, LANES), 0)) < live
        glu_here = [glu_s[h, pl.ds(base + EDGE, rows), :] for h in range(2)]
        acc = [jnp.zeros((rows, LANES), f32) for _ in range(2)]
        for j in range(taps):
            at = pl.ds(base + (2 * EDGE - j), rows)
            same = seg_s[at, :] == here
            for h in range(2):
                value = jnp.where(same, dc_s[h, at, :], 0.0)
                acc[h] = acc[h] + value * w_s[h, j : j + 1, :]
                tap_s[h, j] += jnp.sum((value * glu_here[h]).reshape(rows // BLK, BLK, LANES), axis=0)
        for h in range(2):
            dglu_s[h, pl.ds(base, rows), :] = jnp.where(alive, acc[h], 0.0)
        return carry

    lax.fori_loop(0, blocks, back_body, 0)
    send(1, mixed_s.at[0], mixed_keep_hbm)
    send(2, mixed_s.at[1], mixed_send_hbm)

    per = part // BLK
    parts = grad_ref.shape[0]
    extra = grad_ref.shape[2] - width
    left = parts - 2 * per
    cols = 512
    for d in range(0, width, cols):
        block = dot_general(swish_t, delta_ref[:, d : d + cols], 1, 0).astype(bf16)
        grad_ref[2 * per : parts, :, d : d + cols] = block[0 : left * BLK].reshape(left, BLK, cols)
        over = block[left * BLK :].reshape(per - left, BLK, cols)
        for r in range(per - left):
            for c in range(0, cols, extra):
                at = r * (width // extra) + (d + c) // extra
                grad_ref[at, :, width : width + extra] = over[r, :, c : c + extra]
    first = (per - left) * (width // extra)
    grad_ref[first:parts, :, width : width + extra] = jnp.zeros((parts - first, BLK, extra), bf16)
    for h, (c, e) in enumerate(((0, LANES), (LANES, part))):
        tap = jnp.sum(tap_s[h], axis=1)[:, 0 : e - c].astype(bf16)
        for r in range(taps // BLK):
            grad_ref[first + r, :, width + c : width + e] = tap[r * BLK : (r + 1) * BLK]

    def depart(k, begin, end):
        send(k, grad_ref.at[begin:end], grad_hbm.at[begin:end])

    depart(3, 2 * per, parts)

    for h, (c, e) in enumerate(((0, LANES), (LANES, part))):
        dglu = jnp.transpose(dglu_s[h])[0 : e - c]
        s = sig_s[c:e, :]
        dlt_ref[0, c:e, :] = (dglu * s).astype(bf16)
        dlt_ref[1, c:e, :] = (dglu * lin_s[c:e, :] * s * (1.0 - s)).astype(bf16)


    for k in range(2):
        for d in range(0, width, cols):
            block = dot_general(dlt_ref[k], normed_ref[d : d + cols, :], 1, 1).astype(bf16)
            grad_ref[k * per : (k + 1) * per, :, d : d + cols] = block.reshape(per, BLK, cols)
        depart(4 + k, k * per, (k + 1) * per)

    unit = jnp.zeros((BLK, slots), f32)
    cross = jnp.zeros((BLK, slots), f32)
    wide = 2 * part
    for z in range(chips):
        d = z * wide
        term = dot_general(win_ref[0, :, d : d + wide], dlt_ref[0], 0, 0)
        term = term + dot_general(win_ref[1, :, d : d + wide], dlt_ref[1], 0, 0)
        term = term.astype(bf16)
        first, second = term[0:part], term[part:wide]
        send_ref[z, 0:part, :] = jnp.where(core == 0, second, first)
        send(6 + z, send_ref.at[z, 0:part], send_hbm.at[z, 0:part])
        keep_ref[z, 0:part, :] = jnp.where(core == 0, first, second)
        send(6 + chips + z, keep_ref.at[z, 0:part], keep_hbm.at[z, 0:part])
        weighted = term.astype(f32) * gb_ref[d : d + wide, 0:1]
        standard = (x_ref[d : d + wide, :].astype(f32) - center) * row_scale
        unit = unit + jnp.sum(weighted.reshape(wide // BLK, BLK, slots), axis=0)
        cross = cross + jnp.sum((weighted * standard).reshape(wide // BLK, BLK, slots), axis=0)
    totals = split_rows(
        jnp.sum(unit, axis=0, keepdims=True), jnp.sum(cross, axis=0, keepdims=True)
    )
    for z in range(chips):
        send_ref[z, part : part + SIDE, :] = totals
        keep_ref[z, part : part + SIDE, :] = totals
    below = pl.ds(part, SIDE)
    send(6 + 2 * chips, send_ref.at[:, below], send_hbm.at[:, below])
    send(7 + 2 * chips, keep_ref.at[:, below], keep_hbm.at[:, below])
    for copy in sends:
        copy.wait()


def pair_kernel(scalars, keep_ref, got_ref, *outs):
    chips, rows, _ = keep_ref.shape
    part = rows - SIDE
    side = keep_ref[0, part:rows, :].astype(f32) + got_ref[0, part:rows, :].astype(f32)
    totals = split_rows(side[0:1] + side[1:2], side[2:3] + side[3:4])
    for j in range(chips):
        z = scalars[4] ^ j
        total = keep_ref[z, 0:part, :].astype(f32) + got_ref[z, 0:part, :].astype(f32)
        outs[j][0:part, :] = total.astype(bf16)
        outs[j][part:rows, :] = totals


def sum_kernel(in_ref, out_ref):
    for k in range(out_ref.shape[0]):
        total = sum(in_ref[i, k].astype(f32) for i in range(in_ref.shape[0]))
        out_ref[k] = total.astype(bf16)


def share_kernel(in_ref, home_ref, out_ref):
    peers, _, wide = in_ref.shape
    lines = home_ref.shape[1]
    total = sum(in_ref[i].astype(f32) for i in range(peers)).astype(bf16)
    for i in range(peers):
        out_ref[i, :, 0:wide] = total
        for k in range(lines):
            at = wide + k * 2 * LANES
            out_ref[i, :, at : at + 2 * LANES] = home_ref[i, k]


def unpack_kernel(target, in_ref, weight_ref, out_ref, tap_ref, side_ref, frame_ref, held, turned_rows):
    pieces, _, full = in_ref.shape
    taps, part = tap_ref.shape
    width = weight_ref.shape[1]
    wide = full - 2 * LANES
    extra = wide - width
    per = part // BLK
    left = pieces - 2 * per
    cols = 2 * extra
    for d in range(0, width, cols):
        weight_ref[:, d : d + cols] = in_ref[0 : 2 * per, :, d : d + cols].reshape(2 * part, cols)
        out_ref[0 : left * BLK, d : d + cols] = in_ref[2 * per : pieces, :, d : d + cols].reshape(
            left * BLK, cols
        )
    for c in range(0, width, extra):
        rows = [in_ref[r * (width // extra) + c // extra, :, width:wide] for r in range(per - left)]
        out_ref[left * BLK : part, c : c + extra] = jnp.concatenate(rows, axis=0)
    first = (per - left) * (width // extra)
    for r in range(taps // BLK):
        tap_ref[r * BLK : (r + 1) * BLK, :] = in_ref[first + r, :, width : width + part].astype(f32)
    total = jnp.zeros((BLK, LANES), f32)
    for s in range(pieces):
        held[s] = in_ref[s, :, wide:full].astype(f32)
        total = total + held[s, :, LANES:]
    turned = pltpu.roll(total, LANES - part % LANES, 1)
    low = lax.broadcasted_iota(jnp.int32, (1, LANES), 1) < part % LANES
    for k in range(2):
        side_ref[k : k + 1, 0:LANES] = jnp.where(
            low, turned[3 * k : 3 * k + 1], total[3 * k + 1 : 3 * k + 2]
        )
        side_ref[k : k + 1, LANES:part] = turned[3 * k + 2 : 3 * k + 3, 0 : part - LANES]
    for k in range(frame_ref.shape[1] // BLK):
        turned_rows[k * BLK : (k + 1) * BLK, :] = held[target[k]]
    for c in range(0, part, LANES):
        e = min(part, c + LANES)
        frame_ref[c:e, :] = jnp.transpose(turned_rows[:, c:e]).astype(bf16)


def fan_kernel(in_ref, out_hbm, sems):
    lines, _, _, full = out_hbm.shape
    wide = full - 2 * LANES
    copies = []
    for k in range(lines):
        at = wide + k * 2 * LANES
        to = out_hbm.at[k]
        for n, (source, target) in enumerate(
            (
                (in_ref.at[:, :, 0:wide], to.at[:, :, 0:wide]),
                (in_ref.at[:, :, at : at + 2 * LANES], to.at[:, :, wide:full]),
            )
        ):
            copies.append(pltpu.make_async_copy(source, target, sems.at[2 * k + n]))
    for copy in copies:
        copy.start()
    for copy in copies:
        copy.wait()


def row_kernel(scalars, dn0, dn1, dn2, dn3, x_ref, stats_ref, gain_ref, delta_ref, out_ref, held):
    start, blocks = scalars[0], scalars[1]
    terms = (dn0, dn1, dn2, dn3)
    slots, part = x_ref.shape
    width = scalars[2].astype(f32)
    rest = part - LANES
    count = slots // BLK
    live = blocks * BLK
    totals = sum(term[part : part + SIDE, :].astype(f32) for term in terms)
    unit, cross = totals[0:1] + totals[1:2], totals[2:3] + totals[3:4]
    row = lax.broadcasted_iota(jnp.int32, (BLK, slots), 0)
    side = jnp.where(row == 2, unit, jnp.where(row == 3, cross, stats_ref[...]))
    side = jnp.transpose(side)
    center, row_scale = side[:, 0:1], side[:, 1:2]
    unit, cross = side[:, 2:3] / width, side[:, 3:4] / width
    sums = []
    for h, (c, e) in enumerate(((0, LANES), (LANES, part))):
        dn = jnp.transpose(sum(term[c:e, :].astype(f32) for term in terms))
        standard = (x_ref[:, c:e].astype(f32) - center) * row_scale
        sums.append((jnp.sum(dn * standard, axis=0, keepdims=True), jnp.sum(dn, axis=0, keepdims=True)))
        on = lax.broadcasted_iota(jnp.int32, (slots, e - c), 0) < live
        own = jnp.where(on, delta_ref[:, c:e].astype(f32), 0.0)
        held[h, :, 0 : e - c] = own + row_scale * (dn * gain_ref[:, c:e] - unit - standard * cross)
    held[1, :, rest:LANES] = jnp.zeros((slots, LANES - rest), f32)
    row = lax.broadcasted_iota(jnp.int32, (BLK, LANES), 0)
    lane = lax.broadcasted_iota(jnp.int32, (BLK, LANES), 1)
    beside = jnp.zeros((BLK, LANES), f32)
    for k in range(2):
        low = jnp.broadcast_to(sums[0][k], (BLK, LANES))
        high = jnp.broadcast_to(jnp.concatenate([sums[1][k], sums[1][k]], axis=1), (BLK, LANES))
        beside = jnp.where(row == 3 * k, pltpu.roll(low, 64, 1), beside)
        beside = jnp.where(row == 3 * k + 1, low, beside)
        beside = jnp.where(row == 3 * k + 2, high, beside)
    for s in range(count):
        at = pl.ds(pl.multiple_of(lax.rem(s - start + 16 * count, count) * BLK, BLK), BLK)
        out_ref[s, :, 0:LANES] = held[0, at, :].astype(bf16)
        out_ref[s, :, LANES : 2 * LANES] = jnp.where(lane < rest, held[1, at, :], beside).astype(bf16)


def on_device(
    frames,
    norm_gain,
    norm_bias,
    input_weight,
    depth_weight,
    batch_scale,
    batch_shift,
    output_weight,
    upstream,
    replica_blocks,
    segment,
):
    replicas = lax.axis_size(DP)
    my_index = lax.axis_index(DP)
    tensor_index = lax.axis_index(TENSOR)
    width = norm_gain.shape[0]
    load_rows, part = frames.shape
    slots = segment.shape[0]
    rows_part = upstream.shape[0]
    taps = depth_weight.shape[0]
    load_blocks = load_rows // BLK
    count = slots // BLK

    delta = lax.all_gather(upstream, TENSOR, axis=0, tiled=True)

    ends = jnp.cumsum(replica_blocks)
    starts = ends - replica_blocks
    numbers = my_index + replicas * jnp.arange(load_blocks, dtype=jnp.int32)
    target = jnp.sum((ends[None, :] <= numbers[:, None]).astype(jnp.int32), axis=1)
    is_mine = jnp.arange(replicas, dtype=jnp.int32) == my_index
    my_start = jnp.sum(jnp.where(is_mine, starts, 0))
    my_blocks = jnp.sum(jnp.where(is_mine, replica_blocks, 0))
    core = lax.axis_index("core")
    scalars = jnp.stack([lax.rem(my_start, replicas), my_blocks, jnp.int32(width), core, lax.axis_index("zl")])

    sds = jax.ShapeDtypeStruct
    outbox = full_call(
        outbox_kernel,
        sds((replicas, BLK, part), bf16),
        [
            pltpu.VMEM((load_rows, part), f32),
            pltpu.VMEM((part, load_rows), bf16),
            pltpu.SemaphoreType.DMA(()),
        ],
        2,
        1000,
        400000,
        (2,),
        room=60,
    )(replica_blocks, my_index[None], frames.T)
    arrived = lax.all_to_all(outbox, DP, split_axis=0, concat_axis=0, tiled=True)

    packed, packed_t = full_call(
        pack_kernel,
        (sds((slots, part), bf16), sds((part, slots), bf16)),
        [pltpu.VMEM((slots, part), f32)],
        1,
        1000,
        1000000,
    )(scalars, arrived)
    own = lax.all_gather(packed_t, "zl", axis=0)
    other = lax.ppermute(own, "core", SWAP)
    chips = own.shape[0]

    pieces = replicas
    half = sds((chips, rows_part, width), bf16)
    gathered, keep, send_half, mixed_keep, mixed_send, grads, stats = full_call(
        main_kernel,
        (
            sds((width, slots), bf16),
            sds((chips, part + SIDE, slots), bf16),
            sds((chips, part + SIDE, slots), bf16),
            half,
            half,
            sds((pieces, BLK, width + 2 * LANES), bf16),
            sds((BLK, slots), f32),
        ),
        [
            pltpu.VMEM((width, BLK), f32),
            pltpu.VMEM((2, chips, rows_part, width), bf16),
            pltpu.VMEM((pieces, BLK, width + 2 * LANES), bf16),
            pltpu.VMEM((2, slots + 2 * EDGE, LANES), f32),
            pltpu.VMEM((2, slots + 2 * EDGE, LANES), f32),
            pltpu.VMEM((slots + 2 * EDGE, LANES), f32),
            pltpu.VMEM((2, taps, LANES), f32),
            pltpu.VMEM((2, BLK, LANES), f32),
            pltpu.VMEM((2, slots, LANES), f32),
            pltpu.VMEM((2, slots, LANES), f32),
            pltpu.VMEM((part, slots), f32),
            pltpu.VMEM((part, slots), f32),
            pltpu.VMEM((2, taps, BLK, LANES), f32),
            pltpu.VMEM(own.shape, bf16),
            pltpu.VMEM(other.shape, bf16),
            pltpu.VMEM(input_weight.shape, bf16),
            pltpu.VMEM(delta.shape, bf16),
            pltpu.VMEM(output_weight.shape, bf16),
            pltpu.VMEM((width, slots), bf16),
            pltpu.VMEM((width, slots), bf16),
            pltpu.VMEM((slots, part), bf16),
            pltpu.VMEM((2, part, slots), bf16),
            pltpu.VMEM((chips, part + SIDE, slots), bf16),
            pltpu.VMEM((chips, part + SIDE, slots), bf16),
            pltpu.SemaphoreType.DMA((5,)),
            pltpu.SemaphoreType.DMA((8 + 2 * chips,)),
        ],
        1,
        3000000000,
        12000000,
        (1, 2, 5, 10, 11),
        (0, 1, 2, 3, 4, 5),
        60,
    )(
        scalars,
        own,
        other,
        norm_gain[None],
        norm_bias[None],
        input_weight,
        depth_weight,
        batch_scale[None],
        batch_shift[None],
        segment[None],
        delta,
        output_weight,
    )
    got = lax.ppermute(send_half, "core", SWAP)
    paired = full_call(
        pair_kernel, (sds(keep.shape[1:], bf16),) * chips, [], 1, 1000000, 2400000
    )(scalars, keep, got)
    terms = {0: paired[0]}
    for j in range(chips - 1, 0, -1):
        terms[j] = lax.ppermute(paired[j], "zl", [(z, z ^ j) for z in range(chips)])
    terms = [terms[j] for j in (0, 3, 2, 1)]

    lines, peers = lax.axis_size("x"), lax.axis_size(("zh", "y"))
    grads = grads.reshape((lines, peers) + grads.shape[1:])
    grads = lax.all_to_all(grads, "x", split_axis=0, concat_axis=0, tiled=True)
    grads, *terms = lax.optimization_barrier((grads, *terms))
    grads = full_call(sum_kernel, sds(grads.shape[1:], bf16), [], 0, 1000000, 2300000)(grads)
    grads = lax.all_to_all(grads, ("zh", "y"), split_axis=0, concat_axis=0, tiled=True)

    mixed_send, *terms = lax.optimization_barrier((mixed_send, *terms))
    mixed = mixed_keep.astype(f32) + lax.ppermute(mixed_send, "core", SWAP).astype(f32)
    mixed = mixed.astype(bf16).reshape(chips * rows_part, width)
    mixed_sum = lax.psum_scatter(mixed, "zl", scatter_dimension=0, tiled=True)

    column_start = tensor_index * part
    gain_part = lax.dynamic_slice_in_dim(norm_gain, column_start, part)[None]
    delta_part = lax.dynamic_slice_in_dim(delta, column_start, part, 1)
    homebound = full_call(
        row_kernel,
        sds((count, BLK, 2 * LANES), bf16),
        [pltpu.VMEM((2, slots, LANES), f32)],
        1,
        1000000,
        1000000,
    )(scalars, *terms, packed, stats, gain_part, delta_part)
    wide = grads.shape[-1]
    shared = full_call(
        share_kernel, sds((peers, BLK, wide + lines * 2 * LANES), bf16), [], 0, 1000000, 1500000
    )(grads, homebound.reshape(peers, lines, BLK, 2 * LANES))
    shared = lax.all_to_all(shared, ("zh", "y"), split_axis=0, concat_axis=0, tiled=True)
    fanned, = full_call(
        fan_kernel,
        (sds((lines, peers, BLK, wide + 2 * LANES), bf16),),
        [pltpu.SemaphoreType.DMA((2 * lines,))],
        0,
        1000000,
        3000000,
        (),
        (0,),
        room=16,
    )(shared)
    whole = lax.all_to_all(fanned, "x", split_axis=0, concat_axis=0, tiled=True)
    whole = whole.reshape((pieces,) + whole.shape[2:])
    target = lax.rem(target, lines) * peers + target // lines
    weight_grad, out_grad, tap_grad, side, frame_gradient = full_call(
        unpack_kernel,
        (
            sds((2 * part, width), bf16),
            sds((part, width), bf16),
            sds((taps, part), f32),
            sds((2, part), f32),
            sds((part, load_rows), bf16),
        ),
        [pltpu.VMEM((pieces, BLK, 2 * LANES), f32), pltpu.VMEM((load_rows, 2 * LANES), f32)],
        1,
        1000000,
        5000000,
    )(target, whole)
    weight_grad = weight_grad.reshape(2, part, width)
    frame_gradient = frame_gradient.T

    row_start = tensor_index * rows_part
    live_mine = (row_start + jnp.arange(rows_part, dtype=jnp.int32) < my_blocks * BLK)[:, None]
    residual = lax.dynamic_slice_in_dim(gathered, row_start, rows_part, 1).T
    block_output = jnp.where(
        live_mine, residual.astype(f32) + mixed_sum.astype(f32), 0.0
    ).astype(bf16)
    return (block_output, frame_gradient, weight_grad, out_grad, tap_grad, side[0], side[1])


def solution(mesh):
    fine = Mesh(mesh.devices.reshape(2, 8, 4, 4, 2), DP + TENSOR)
    in_specs = (
        P(DP, TENSOR),
        P(),
        P(),
        P(None, TENSOR, None),
        P(None, TENSOR),
        P(TENSOR),
        P(TENSOR),
        P(TENSOR, None),
        P(DP + TENSOR, None),
        P(),
        P(DP),
    )
    out_specs = (
        P(DP + TENSOR, None),
        P(DP, TENSOR),
        P(None, TENSOR, None),
        P(TENSOR, None),
        P(None, TENSOR),
        P(TENSOR),
        P(TENSOR),
    )
    return jax.shard_map(
        on_device, mesh=fine, in_specs=in_specs, out_specs=out_specs, check_vma=False
    )
```

```python
import functools

import jax
import jax.numpy as jnp
from jax import lax
from jax.experimental import pallas as pl
from jax.experimental.pallas import tpu as pltpu
from jax.sharding import Mesh
from jax.sharding import PartitionSpec as P

BLK = 8
LANES = 128
EDGE = 16
SIDE = 16
epsilon = 1e-05
MIB = 1024 * 1024

f32 = jnp.float32
bf16 = jnp.bfloat16
SWAP = ((0, 1), (1, 0))
DP = ("zh", "y", "x")
TENSOR = ("zl", "core")


def dot_general(a, b, ca, cb):
    return lax.dot_general(a, b, (((ca,), (cb,)), ((), ())), preferred_element_type=f32)


def full_call(kernel, out_shape, scratch, smem, flops, nbytes, copied=(), sent=(), room=16):
    def call(*args):
        specs = [pl.BlockSpec(memory_space=pltpu.SMEM)] * smem
        specs += [pl.BlockSpec(memory_space=pltpu.VMEM)] * (len(args) - smem)
        for place in copied:
            specs[place] = pl.BlockSpec(memory_space=pltpu.HBM)
        outs = jax.tree.map(lambda _: pl.BlockSpec(memory_space=pltpu.VMEM), out_shape)
        if sent:
            outs = tuple(
                pl.BlockSpec(memory_space=pltpu.HBM if k in sent else pltpu.VMEM)
                for k in range(len(out_shape))
            )
        return pl.pallas_call(
            kernel,
            out_shape=out_shape,
            in_specs=specs,
            out_specs=outs,
            scratch_shapes=scratch,
            compiler_params=pltpu.CompilerParams(vmem_limit_bytes=room * MIB),
            cost_estimate=pl.CostEstimate(flops=flops, bytes_accessed=nbytes, transcendentals=0),
        )(*args)

    return call


def outbox_kernel(replica_blocks, place, frames_hbm, out_ref, held, frames_t, sem):
    copy = pltpu.make_async_copy(frames_hbm, frames_t, sem)
    copy.start()
    part, rows = frames_t.shape
    count = out_ref.shape[0]
    copy.wait()
    for c in range(0, part, LANES):
        e = min(part, c + LANES)
        held[:, c:e] = jnp.transpose(frames_t[c:e, :].astype(f32))
    start = jnp.int32(0)
    for r in range(count):
        block = jnp.minimum(lax.div(start - place[0] + (count - 1), count), rows // BLK - 1)
        at = pl.ds(pl.multiple_of(block * BLK, BLK), BLK)
        out_ref[r] = held[at, :].astype(bf16)
        start = start + replica_blocks[r]


def pack_kernel(scalars, arrived, rows_out, cols_out, held):
    start, blocks = scalars[0], scalars[1]
    count, _, width = arrived.shape
    for p in range(count):
        block = arrived[lax.rem(start + p, count)].astype(f32)
        held[p * BLK : (p + 1) * BLK, :] = jnp.where(p < blocks, block, 0.0)
    rows = held[...]
    rows_out[...] = rows.astype(bf16)
    for c in range(0, width, LANES):
        e = min(width, c + LANES)
        cols_out[c:e, :] = jnp.transpose(held[:, c:e]).astype(bf16)


def split_rows(unit, cross):
    row = lax.broadcasted_iota(jnp.int32, (SIDE, unit.shape[1]), 0)
    out = jnp.zeros((SIDE, unit.shape[1]), f32)
    for k, value in enumerate((unit, cross)):
        high = value.astype(bf16).astype(f32)
        out = jnp.where(row == 2 * k, high, out)
        out = jnp.where(row == 2 * k + 1, value - high, out)
    return out.astype(bf16)


def main_kernel(
    scalars,
    own_hbm,
    other_hbm,
    gain_ref,
    bias_ref,
    win_hbm,
    taps_ref,
    scale_ref,
    shift_ref,
    seg_ref,
    delta_hbm,
    wout_hbm,
    x_hbm,
    keep_hbm,
    send_hbm,
    mixed_keep_hbm,
    mixed_send_hbm,
    grad_hbm,
    stats_ref,
    gb_ref,
    mixed_s,
    grad_ref,
    glu_s,
    dc_s,
    seg_s,
    w_s,
    bn_s,
    pre_s,
    dglu_s,
    lin_s,
    sig_s,
    tap_s,
    own_ref,
    other_ref,
    win_ref,
    delta_ref,
    wout_ref,
    x_ref,
    normed_ref,
    swish_ref,
    dlt_ref,
    keep_ref,
    send_ref,
    sems,
    out_sems,
):
    def send(k, source, target):
        copy = pltpu.make_async_copy(source, target, out_sems.at[k])
        copy.start()
        sends.append(copy)

    sends = []
    copies = [
        pltpu.make_async_copy(source, target, sems.at[k])
        for k, (source, target) in enumerate(
            (
                (own_hbm, own_ref),
                (other_hbm, other_ref),
                (win_hbm, win_ref),
                (delta_hbm, delta_ref),
                (wout_hbm, wout_ref),
            )
        )
    ]
    for copy in copies:
        copy.start()
    width, slots = x_ref.shape
    part = win_ref.shape[1]
    taps = taps_ref.shape[0]
    rest = part - LANES
    live = scalars[1] * BLK
    core = scalars[3]
    chunk = 64
    steps = width // chunk
    chips = own_ref.shape[0]
    per_part = part // chunk

    w_s[...] = jnp.zeros_like(w_s)
    w_s[0] = taps_ref[:, 0:LANES]
    w_s[1, :, 0:rest] = taps_ref[:, LANES:part]
    bn_s[...] = jnp.zeros_like(bn_s)
    bn_s[0, 0:1, :] = scale_ref[:, 0:LANES]
    bn_s[1, 0:1, 0:rest] = scale_ref[:, LANES:part]
    bn_s[0, 1:2, :] = shift_ref[:, 0:LANES]
    bn_s[1, 1:2, 0:rest] = shift_ref[:, LANES:part]
    row = lax.broadcasted_iota(jnp.int32, (BLK, width), 0)
    gb_ref[...] = jnp.transpose(jnp.where(row == 0, gain_ref[...], bias_ref[...]))
    segments = jnp.broadcast_to(seg_ref[...].astype(f32), (BLK, slots))
    seg_s[...] = jnp.full(seg_s.shape, -1.0, f32)
    seg_s[EDGE : EDGE + slots, :] = jnp.broadcast_to(jnp.transpose(segments)[:, 0:1], (slots, LANES))

    glu_s[...] = jnp.zeros_like(glu_s)
    dc_s[...] = jnp.zeros_like(dc_s)
    tap_s[...] = jnp.zeros_like(tap_s)

    copies[0].wait()
    copies[1].wait()

    def fold(v):
        return jnp.sum(v.reshape(chunk // BLK, BLK, slots), axis=0)

    def sum_body(i, acc):
        chip, row = i // per_part, pl.multiple_of(lax.rem(i, per_part) * chunk, chunk)
        for ref, c in ((own_ref, core), (other_ref, 1 - core)):
            value = ref[chip, pl.ds(row, chunk), :]
            to = pl.multiple_of((2 * chip + c) * part + row, chunk)
            x_ref[pl.ds(to, chunk), :] = value
            acc = acc + fold(value.astype(f32))
        return acc

    zero = jnp.zeros((BLK, slots), f32)
    center = lax.fori_loop(0, chips * per_part, sum_body, zero, unroll=3)
    center = jnp.sum(center, axis=0, keepdims=True) / width

    send(0, x_ref, x_hbm)

    def square_body(i, acc):
        return acc + fold(jnp.square(x_ref[pl.ds(i * chunk, chunk), :].astype(f32) - center))

    spread = jnp.sum(lax.fori_loop(0, steps, square_body, zero, unroll=12), axis=0, keepdims=True) / width
    row_scale = lax.rsqrt(spread + epsilon)
    stats_ref[...] = jnp.zeros_like(stats_ref)
    stats_ref[0:1, :] = center
    stats_ref[1:2, :] = row_scale

    def norm_body(i, carry):
        at = pl.ds(i * chunk, chunk)
        standard = (x_ref[at, :].astype(f32) - center) * row_scale
        normed_ref[at, :] = (standard * gb_ref[at, 0:1] + gb_ref[at, 1:2]).astype(bf16)
        return carry

    lax.fori_loop(0, steps, norm_body, 0, unroll=12)


    copies[2].wait()
    normed = normed_ref[...]
    linear = dot_general(win_ref[0], normed, 1, 0)
    gate_sigmoid = jax.nn.sigmoid(dot_general(win_ref[1], normed, 1, 0))
    lin_s[...] = linear
    sig_s[...] = gate_sigmoid
    is_live = lax.broadcasted_iota(jnp.int32, (part, slots), 1) < live
    glu = jnp.where(is_live, (linear * gate_sigmoid).astype(bf16).astype(f32), 0.0)
    glu_s[0, EDGE : EDGE + slots, :] = jnp.transpose(glu[0:LANES])
    glu_s[1, EDGE : EDGE + slots, 0:rest] = jnp.transpose(glu[LANES:part])

    rows = 64
    blocks = slots // rows
    copies[3].wait()
    copies[4].wait()

    tall = 2 * rows

    def conv_body(i, carry):
        base = pl.multiple_of(i * tall, tall)
        here = seg_s[pl.ds(base + EDGE, tall), :]
        acc = [jnp.zeros((tall, LANES), f32) for _ in range(2)]
        for j in range(taps):
            same = seg_s[pl.ds(base + j, tall), :] == here
            for h in range(2):
                value = jnp.where(same, glu_s[h, pl.ds(base + j, tall), :], 0.0)
                acc[h] = acc[h] + value * w_s[h, j : j + 1, :]
        for h in range(2):
            pre_s[h, pl.ds(base, tall), :] = acc[h] * bn_s[h, 0:1, :] + bn_s[h, 1:2, :]
        return carry

    lax.fori_loop(0, slots // tall, conv_body, 0)

    delta_swish = dot_general(delta_ref[...], wout_ref[...], 1, 1)
    row_live = lax.broadcasted_iota(jnp.int32, (slots, LANES), 0) < live
    for h in range(2):
        pre = pre_s[h]
        s = jax.nn.sigmoid(pre)
        swish = jnp.where(row_live, pre * s, 0.0).astype(bf16)
        slope = jnp.where(row_live, s * (1.0 + pre * (1.0 - s)) * bn_s[h, 0:1, :], 0.0)
        if h == 0:
            swish_ref[:, 0:LANES] = swish
            dc_s[h, EDGE : EDGE + slots, :] = delta_swish[:, 0:LANES] * slope
        else:
            swish_ref[:, LANES:part] = swish[:, 0:rest]
            dc_s[h, EDGE : EDGE + slots, 0:rest] = delta_swish[:, LANES:part] * slope[:, 0:rest]

    swish_t = jnp.transpose(swish_ref[...].astype(f32)).astype(bf16)


    def back_body(i, carry):
        base = pl.multiple_of(i * rows, rows)
        mixed = dot_general(swish_ref[pl.ds(base, rows), :], wout_ref[...], 1, 0)
        mixed_s[lax.rem(i, 2) ^ core, i // 2] = mixed.astype(bf16)
        here = seg_s[pl.ds(base + EDGE, rows), :]
        alive = (base + lax.broadcasted_iota(jnp.int32, (rows, LANES), 0)) < live
        glu_here = [glu_s[h, pl.ds(base + EDGE, rows), :] for h in range(2)]
        acc = [jnp.zeros((rows, LANES), f32) for _ in range(2)]
        for j in range(taps):
            at = pl.ds(base + (2 * EDGE - j), rows)
            same = seg_s[at, :] == here
            for h in range(2):
                value = jnp.where(same, dc_s[h, at, :], 0.0)
                acc[h] = acc[h] + value * w_s[h, j : j + 1, :]
                tap_s[h, j] += jnp.sum((value * glu_here[h]).reshape(rows // BLK, BLK, LANES), axis=0)
        for h in range(2):
            dglu_s[h, pl.ds(base, rows), :] = jnp.where(alive, acc[h], 0.0)
        return carry

    lax.fori_loop(0, blocks, back_body, 0)
    send(1, mixed_s.at[0], mixed_keep_hbm)
    send(2, mixed_s.at[1], mixed_send_hbm)

    per = part // BLK
    parts = grad_ref.shape[0]
    extra = grad_ref.shape[2] - width
    left = parts - 2 * per
    cols = 512
    for d in range(0, width, cols):
        block = dot_general(swish_t, delta_ref[:, d : d + cols], 1, 0).astype(bf16)
        grad_ref[2 * per : parts, :, d : d + cols] = block[0 : left * BLK].reshape(left, BLK, cols)
        over = block[left * BLK :].reshape(per - left, BLK, cols)
        for r in range(per - left):
            for c in range(0, cols, extra):
                at = r * (width // extra) + (d + c) // extra
                grad_ref[at, :, width : width + extra] = over[r, :, c : c + extra]
    first = (per - left) * (width // extra)
    grad_ref[first:parts, :, width : width + extra] = jnp.zeros((parts - first, BLK, extra), bf16)
    for h, (c, e) in enumerate(((0, LANES), (LANES, part))):
        tap = jnp.sum(tap_s[h], axis=1)[:, 0 : e - c].astype(bf16)
        for r in range(taps // BLK):
            grad_ref[first + r, :, width + c : width + e] = tap[r * BLK : (r + 1) * BLK]

    def depart(k, begin, end):
        send(k, grad_ref.at[begin:end], grad_hbm.at[begin:end])

    depart(3, 2 * per, parts)

    for h, (c, e) in enumerate(((0, LANES), (LANES, part))):
        dglu = jnp.transpose(dglu_s[h])[0 : e - c]
        s = sig_s[c:e, :]
        dlt_ref[0, c:e, :] = (dglu * s).astype(bf16)
        dlt_ref[1, c:e, :] = (dglu * lin_s[c:e, :] * s * (1.0 - s)).astype(bf16)


    for k in range(2):
        for d in range(0, width, cols):
            block = dot_general(dlt_ref[k], normed_ref[d : d + cols, :], 1, 1).astype(bf16)
            grad_ref[k * per : (k + 1) * per, :, d : d + cols] = block.reshape(per, BLK, cols)
        depart(4 + k, k * per, (k + 1) * per)

    unit = jnp.zeros((BLK, slots), f32)
    cross = jnp.zeros((BLK, slots), f32)
    wide = 2 * part
    for z in range(chips):
        d = z * wide
        term = dot_general(win_ref[0, :, d : d + wide], dlt_ref[0], 0, 0)
        term = term + dot_general(win_ref[1, :, d : d + wide], dlt_ref[1], 0, 0)
        term = term.astype(bf16)
        first, second = term[0:part], term[part:wide]
        send_ref[z, 0:part, :] = jnp.where(core == 0, second, first)
        send(6 + z, send_ref.at[z, 0:part], send_hbm.at[z, 0:part])
        keep_ref[z, 0:part, :] = jnp.where(core == 0, first, second)
        send(6 + chips + z, keep_ref.at[z, 0:part], keep_hbm.at[z, 0:part])
        weighted = term.astype(f32) * gb_ref[d : d + wide, 0:1]
        standard = (x_ref[d : d + wide, :].astype(f32) - center) * row_scale
        unit = unit + jnp.sum(weighted.reshape(wide // BLK, BLK, slots), axis=0)
        cross = cross + jnp.sum((weighted * standard).reshape(wide // BLK, BLK, slots), axis=0)
    totals = split_rows(
        jnp.sum(unit, axis=0, keepdims=True), jnp.sum(cross, axis=0, keepdims=True)
    )
    for z in range(chips):
        send_ref[z, part : part + SIDE, :] = totals
        keep_ref[z, part : part + SIDE, :] = totals
    below = pl.ds(part, SIDE)
    send(6 + 2 * chips, send_ref.at[:, below], send_hbm.at[:, below])
    send(7 + 2 * chips, keep_ref.at[:, below], keep_hbm.at[:, below])
    for copy in sends:
        copy.wait()


def pair_kernel(scalars, keep_ref, got_ref, *outs):
    chips, rows, _ = keep_ref.shape
    part = rows - SIDE
    side = keep_ref[0, part:rows, :].astype(f32) + got_ref[0, part:rows, :].astype(f32)
    totals = split_rows(side[0:1] + side[1:2], side[2:3] + side[3:4])
    for j in range(chips):
        z = scalars[4] ^ j
        total = keep_ref[z, 0:part, :].astype(f32) + got_ref[z, 0:part, :].astype(f32)
        outs[j][0:part, :] = total.astype(bf16)
        outs[j][part:rows, :] = totals


def sum_kernel(in_ref, out_ref):
    for k in range(out_ref.shape[0]):
        total = sum(in_ref[i, k].astype(f32) for i in range(in_ref.shape[0]))
        out_ref[k] = total.astype(bf16)


def share_kernel(in_ref, home_ref, out_ref):
    peers, _, wide = in_ref.shape
    lines = home_ref.shape[1]
    total = sum(in_ref[i].astype(f32) for i in range(peers)).astype(bf16)
    for i in range(peers):
        out_ref[i, :, 0:wide] = total
        for k in range(lines):
            at = wide + k * 2 * LANES
            out_ref[i, :, at : at + 2 * LANES] = home_ref[i, k]


def unpack_kernel(target, in_ref, weight_ref, out_ref, tap_ref, side_ref, frame_ref, held, turned_rows):
    pieces, _, full = in_ref.shape
    taps, part = tap_ref.shape
    width = weight_ref.shape[1]
    wide = full - 2 * LANES
    extra = wide - width
    per = part // BLK
    left = pieces - 2 * per
    cols = 2 * extra
    for d in range(0, width, cols):
        weight_ref[:, d : d + cols] = in_ref[0 : 2 * per, :, d : d + cols].reshape(2 * part, cols)
        out_ref[0 : left * BLK, d : d + cols] = in_ref[2 * per : pieces, :, d : d + cols].reshape(
            left * BLK, cols
        )
    for c in range(0, width, extra):
        rows = [in_ref[r * (width // extra) + c // extra, :, width:wide] for r in range(per - left)]
        out_ref[left * BLK : part, c : c + extra] = jnp.concatenate(rows, axis=0)
    first = (per - left) * (width // extra)
    for r in range(taps // BLK):
        tap_ref[r * BLK : (r + 1) * BLK, :] = in_ref[first + r, :, width : width + part].astype(f32)
    total = jnp.zeros((BLK, LANES), f32)
    for s in range(pieces):
        held[s] = in_ref[s, :, wide:full].astype(f32)
        total = total + held[s, :, LANES:]
    turned = pltpu.roll(total, LANES - part % LANES, 1)
    low = lax.broadcasted_iota(jnp.int32, (1, LANES), 1) < part % LANES
    for k in range(2):
        side_ref[k : k + 1, 0:LANES] = jnp.where(
            low, turned[3 * k : 3 * k + 1], total[3 * k + 1 : 3 * k + 2]
        )
        side_ref[k : k + 1, LANES:part] = turned[3 * k + 2 : 3 * k + 3, 0 : part - LANES]
    for k in range(frame_ref.shape[1] // BLK):
        turned_rows[k * BLK : (k + 1) * BLK, :] = held[target[k]]
    for c in range(0, part, LANES):
        e = min(part, c + LANES)
        frame_ref[c:e, :] = jnp.transpose(turned_rows[:, c:e]).astype(bf16)


def fan_kernel(in_ref, out_hbm, sems):
    lines, _, _, full = out_hbm.shape
    wide = full - 2 * LANES
    copies = []
    for k in range(lines):
        at = wide + k * 2 * LANES
        to = out_hbm.at[k]
        for n, (source, target) in enumerate(
            (
                (in_ref.at[:, :, 0:wide], to.at[:, :, 0:wide]),
                (in_ref.at[:, :, at : at + 2 * LANES], to.at[:, :, wide:full]),
            )
        ):
            copies.append(pltpu.make_async_copy(source, target, sems.at[2 * k + n]))
    for copy in copies:
        copy.start()
    for copy in copies:
        copy.wait()


def row_kernel(scalars, dn0, dn1, dn2, dn3, x_ref, stats_ref, gain_ref, delta_ref, out_ref, held):
    start, blocks = scalars[0], scalars[1]
    terms = (dn0, dn1, dn2, dn3)
    slots, part = x_ref.shape
    width = scalars[2].astype(f32)
    rest = part - LANES
    count = slots // BLK
    live = blocks * BLK
    totals = sum(term[part : part + SIDE, :].astype(f32) for term in terms)
    unit, cross = totals[0:1] + totals[1:2], totals[2:3] + totals[3:4]
    row = lax.broadcasted_iota(jnp.int32, (BLK, slots), 0)
    side = jnp.where(row == 2, unit, jnp.where(row == 3, cross, stats_ref[...]))
    side = jnp.transpose(side)
    center, row_scale = side[:, 0:1], side[:, 1:2]
    unit, cross = side[:, 2:3] / width, side[:, 3:4] / width
    sums = []
    for h, (c, e) in enumerate(((0, LANES), (LANES, part))):
        dn = jnp.transpose(sum(term[c:e, :].astype(f32) for term in terms))
        standard = (x_ref[:, c:e].astype(f32) - center) * row_scale
        sums.append((jnp.sum(dn * standard, axis=0, keepdims=True), jnp.sum(dn, axis=0, keepdims=True)))
        on = lax.broadcasted_iota(jnp.int32, (slots, e - c), 0) < live
        own = jnp.where(on, delta_ref[:, c:e].astype(f32), 0.0)
        held[h, :, 0 : e - c] = own + row_scale * (dn * gain_ref[:, c:e] - unit - standard * cross)
    held[1, :, rest:LANES] = jnp.zeros((slots, LANES - rest), f32)
    row = lax.broadcasted_iota(jnp.int32, (BLK, LANES), 0)
    lane = lax.broadcasted_iota(jnp.int32, (BLK, LANES), 1)
    beside = jnp.zeros((BLK, LANES), f32)
    for k in range(2):
        low = jnp.broadcast_to(sums[0][k], (BLK, LANES))
        high = jnp.broadcast_to(jnp.concatenate([sums[1][k], sums[1][k]], axis=1), (BLK, LANES))
        beside = jnp.where(row == 3 * k, pltpu.roll(low, 64, 1), beside)
        beside = jnp.where(row == 3 * k + 1, low, beside)
        beside = jnp.where(row == 3 * k + 2, high, beside)
    for s in range(count):
        at = pl.ds(pl.multiple_of(lax.rem(s - start + 16 * count, count) * BLK, BLK), BLK)
        out_ref[s, :, 0:LANES] = held[0, at, :].astype(bf16)
        out_ref[s, :, LANES : 2 * LANES] = jnp.where(lane < rest, held[1, at, :], beside).astype(bf16)


def on_device(
    frames,
    norm_gain,
    norm_bias,
    input_weight,
    depth_weight,
    batch_scale,
    batch_shift,
    output_weight,
    upstream,
    replica_blocks,
    segment,
):
    replicas = lax.axis_size(DP)
    my_index = lax.axis_index(DP)
    tensor_index = lax.axis_index(TENSOR)
    width = norm_gain.shape[0]
    load_rows, part = frames.shape
    slots = segment.shape[0]
    rows_part = upstream.shape[0]
    taps = depth_weight.shape[0]
    load_blocks = load_rows // BLK
    count = slots // BLK

    delta = lax.all_gather(upstream, TENSOR, axis=0, tiled=True)

    ends = jnp.cumsum(replica_blocks)
    starts = ends - replica_blocks
    numbers = my_index + replicas * jnp.arange(load_blocks, dtype=jnp.int32)
    target = jnp.sum((ends[None, :] <= numbers[:, None]).astype(jnp.int32), axis=1)
    is_mine = jnp.arange(replicas, dtype=jnp.int32) == my_index
    my_start = jnp.sum(jnp.where(is_mine, starts, 0))
    my_blocks = jnp.sum(jnp.where(is_mine, replica_blocks, 0))
    core = lax.axis_index("core")
    scalars = jnp.stack([lax.rem(my_start, replicas), my_blocks, jnp.int32(width), core, lax.axis_index("zl")])

    sds = jax.ShapeDtypeStruct
    outbox = full_call(
        outbox_kernel,
        sds((replicas, BLK, part), bf16),
        [
            pltpu.VMEM((load_rows, part), f32),
            pltpu.VMEM((part, load_rows), bf16),
            pltpu.SemaphoreType.DMA(()),
        ],
        2,
        1000,
        400000,
        (2,),
        room=60,
    )(replica_blocks, my_index[None], frames.T)
    arrived = lax.all_to_all(outbox, DP, split_axis=0, concat_axis=0, tiled=True)

    packed, packed_t = full_call(
        pack_kernel,
        (sds((slots, part), bf16), sds((part, slots), bf16)),
        [pltpu.VMEM((slots, part), f32)],
        1,
        1000,
        1000000,
    )(scalars, arrived)
    own = lax.all_gather(packed_t, "zl", axis=0)
    other = lax.ppermute(own, "core", SWAP)
    chips = own.shape[0]

    pieces = replicas
    half = sds((chips, rows_part, width), bf16)
    gathered, keep, send_half, mixed_keep, mixed_send, grads, stats = full_call(
        main_kernel,
        (
            sds((width, slots), bf16),
            sds((chips, part + SIDE, slots), bf16),
            sds((chips, part + SIDE, slots), bf16),
            half,
            half,
            sds((pieces, BLK, width + 2 * LANES), bf16),
            sds((BLK, slots), f32),
        ),
        [
            pltpu.VMEM((width, BLK), f32),
            pltpu.VMEM((2, chips, rows_part, width), bf16),
            pltpu.VMEM((pieces, BLK, width + 2 * LANES), bf16),
            pltpu.VMEM((2, slots + 2 * EDGE, LANES), f32),
            pltpu.VMEM((2, slots + 2 * EDGE, LANES), f32),
            pltpu.VMEM((slots + 2 * EDGE, LANES), f32),
            pltpu.VMEM((2, taps, LANES), f32),
            pltpu.VMEM((2, BLK, LANES), f32),
            pltpu.VMEM((2, slots, LANES), f32),
            pltpu.VMEM((2, slots, LANES), f32),
            pltpu.VMEM((part, slots), f32),
            pltpu.VMEM((part, slots), f32),
            pltpu.VMEM((2, taps, BLK, LANES), f32),
            pltpu.VMEM(own.shape, bf16),
            pltpu.VMEM(other.shape, bf16),
            pltpu.VMEM(input_weight.shape, bf16),
            pltpu.VMEM(delta.shape, bf16),
            pltpu.VMEM(output_weight.shape, bf16),
            pltpu.VMEM((width, slots), bf16),
            pltpu.VMEM((width, slots), bf16),
            pltpu.VMEM((slots, part), bf16),
            pltpu.VMEM((2, part, slots), bf16),
            pltpu.VMEM((chips, part + SIDE, slots), bf16),
            pltpu.VMEM((chips, part + SIDE, slots), bf16),
            pltpu.SemaphoreType.DMA((5,)),
            pltpu.SemaphoreType.DMA((8 + 2 * chips,)),
        ],
        1,
        3000000000,
        12000000,
        (1, 2, 5, 10, 11),
        (0, 1, 2, 3, 4, 5),
        60,
    )(
        scalars,
        own,
        other,
        norm_gain[None],
        norm_bias[None],
        input_weight,
        depth_weight,
        batch_scale[None],
        batch_shift[None],
        segment[None],
        delta,
        output_weight,
    )
    got = lax.ppermute(send_half, "core", SWAP)
    paired = full_call(
        pair_kernel, (sds(keep.shape[1:], bf16),) * chips, [], 1, 1000000, 2400000
    )(scalars, keep, got)
    terms = {0: paired[0]}
    for j in range(chips - 1, 0, -1):
        terms[j] = lax.ppermute(paired[j], "zl", [(z, z ^ j) for z in range(chips)])
    terms = [terms[j] for j in (0, 3, 2, 1)]

    lines, peers = lax.axis_size("x"), lax.axis_size(("zh", "y"))
    grads = grads.reshape((lines, peers) + grads.shape[1:])
    grads = lax.all_to_all(grads, "x", split_axis=0, concat_axis=0, tiled=True)
    grads, *terms = lax.optimization_barrier((grads, *terms))
    grads = full_call(sum_kernel, sds(grads.shape[1:], bf16), [], 0, 1000000, 2300000)(grads)
    grads = lax.all_to_all(grads, ("zh", "y"), split_axis=0, concat_axis=0, tiled=True)

    mixed_send, *terms = lax.optimization_barrier((mixed_send, *terms))
    mixed = mixed_keep.astype(f32) + lax.ppermute(mixed_send, "core", SWAP).astype(f32)
    mixed = mixed.astype(bf16).reshape(chips * rows_part, width)
    mixed_sum = lax.psum_scatter(mixed, "zl", scatter_dimension=0, tiled=True)

    column_start = tensor_index * part
    gain_part = lax.dynamic_slice_in_dim(norm_gain, column_start, part)[None]
    delta_part = lax.dynamic_slice_in_dim(delta, column_start, part, 1)
    homebound = full_call(
        row_kernel,
        sds((count, BLK, 2 * LANES), bf16),
        [pltpu.VMEM((2, slots, LANES), f32)],
        1,
        1000000,
        1000000,
    )(scalars, *terms, packed, stats, gain_part, delta_part)
    wide = grads.shape[-1]
    shared = full_call(
        share_kernel, sds((peers, BLK, wide + lines * 2 * LANES), bf16), [], 0, 1000000, 1500000
    )(grads, homebound.reshape(peers, lines, BLK, 2 * LANES))
    shared = lax.all_to_all(shared, ("zh", "y"), split_axis=0, concat_axis=0, tiled=True)
    fanned, = full_call(
        fan_kernel,
        (sds((lines, peers, BLK, wide + 2 * LANES), bf16),),
        [pltpu.SemaphoreType.DMA((2 * lines,))],
        0,
        1000000,
        3000000,
        (),
        (0,),
        room=16,
    )(shared)
    whole = lax.all_to_all(fanned, "x", split_axis=0, concat_axis=0, tiled=True)
    whole = whole.reshape((pieces,) + whole.shape[2:])
    target = lax.rem(target, lines) * peers + target // lines
    weight_grad, out_grad, tap_grad, side, frame_gradient = full_call(
        unpack_kernel,
        (
            sds((2 * part, width), bf16),
            sds((part, width), bf16),
            sds((taps, part), f32),
            sds((2, part), f32),
            sds((part, load_rows), bf16),
        ),
        [pltpu.VMEM((pieces, BLK, 2 * LANES), f32), pltpu.VMEM((load_rows, 2 * LANES), f32)],
        1,
        1000000,
        5000000,
    )(target, whole)
    weight_grad = weight_grad.reshape(2, part, width)
    frame_gradient = frame_gradient.T

    row_start = tensor_index * rows_part
    live_mine = (row_start + jnp.arange(rows_part, dtype=jnp.int32) < my_blocks * BLK)[:, None]
    residual = lax.dynamic_slice_in_dim(gathered, row_start, rows_part, 1).T
    block_output = jnp.where(
        live_mine, residual.astype(f32) + mixed_sum.astype(f32), 0.0
    ).astype(bf16)
    return (block_output, frame_gradient, weight_grad, out_grad, tap_grad, side[0], side[1])


def solution(mesh):
    fine = Mesh(mesh.devices.reshape(2, 8, 4, 4, 2), DP + TENSOR)
    in_specs = (
        P(DP, TENSOR),
        P(),
        P(),
        P(None, TENSOR, None),
        P(None, TENSOR),
        P(TENSOR),
        P(TENSOR),
        P(TENSOR, None),
        P(DP + TENSOR, None),
        P(),
        P(DP),
    )
    out_specs = (
        P(DP + TENSOR, None),
        P(DP, TENSOR),
        P(None, TENSOR, None),
        P(TENSOR, None),
        P(None, TENSOR),
        P(TENSOR),
        P(TENSOR),
    )
    return jax.shard_map(
        on_device, mesh=fine, in_specs=in_specs, out_specs=out_specs, check_vma=False
    )
```
